128 devices in a mesh: dp: 32 (over x, z, core), mp: 4 (over y).
Axes of the slice: x: 4, y: 4, z: 4, core: 2. Of those that a mesh axis runs over, the one named last changes fastest.
Arguments:
- delays: float32 [262144], P('dp'), may hold values from -6 to 6
- kernel_tiles: bfloat16 [32, 4, 256, 128, 128], P('dp', 'mp'), may hold values from -0.09375 to 0.09375
- row_blocks: int32 [32, 4, 256], P('dp', 'mp'), may hold values from 0 to 63
- col_blocks: int32 [32, 4, 256], P('dp', 'mp'), may hold values from 0 to 4095
- tile_counts: int32 [32, 4], P('dp', 'mp'), may hold values from 64 to 256, as said below
Outputs:
- slowness: float32 [2097152], P('mp')
- left_dir: float32 [262144], P('dp')
The draws below stay inside these ranges and needn't reach their ends.
Inputs may be any that keep to these rules, and one draw needn't show every extreme that they name: tile_counts[d, m] is the number of leading live tile slots of device (d, m); some device is full in every draw.
All inputs are finite; a program needn't handle non-finite values.
Results may differ from the reference program's by a relative error of at most 0.0076.
Values sent between devices are 32-bit elements; how exact they have to be, the bound alone decides.
A program may use at most 64 MiB of HBM per device.

```python
import jax
import jax.numpy as jnp
from jax import lax

TILE = 128
RB_DEV = 64
CB_DEV = 4096
KT = 256
ITERS = 2
DATA_GROUPS = 32
MODEL_GROUPS = 4
NROWS = 262144
NCELLS = 2097152


def draw_tile_counts(key, part):
    key = jax.random.fold_in(key, 7)
    first_key, second_key = jax.random.split(key)
    counts_all = jax.random.randint(first_key, (DATA_GROUPS * MODEL_GROUPS,), KT // 4, KT + 1, dtype=jnp.int32)
    position = jax.random.randint(second_key, (), 0, DATA_GROUPS * MODEL_GROUPS, dtype=jnp.int32)
    counts_all = counts_all.at[position].set(KT)
    return counts_all.reshape(DATA_GROUPS, MODEL_GROUPS)


def plant(values, key, least, top_value):
    extent = values.shape
    index_at = [jax.random.randint(jax.random.fold_in(key, axis), (), 0, extent[axis]) for axis in range(len(extent))]
    values = values.at[tuple(index_at)].set(least)
    longest = extent.index(max(extent))
    index_at[longest] = (index_at[longest] + 1) % extent[longest]
    return values.at[tuple(index_at)].set(top_value)


def block_levels(stream_key, dims, cuts, least, largest):
    def one(dim, shards_of):
        heights = jax.random.uniform(jax.random.fold_in(jax.random.fold_in(stream_key, 6), dim), (shards_of,), jnp.float32, least / len(cuts), largest / len(cuts))
        return jnp.repeat(jnp.exp(heights), dims[dim] // shards_of).reshape((-1,) + (1,) * (len(dims) - dim - 1))

    level = one(*cuts[0])
    for cut in cuts[1:]:
        level = level * one(*cut)
    return level


def scatter_about(stream_key, extent, deviation, most, cuts=(), held_as=jnp.bfloat16):
    drawn = jax.random.normal(stream_key, extent, jnp.float32) * deviation
    if len(cuts) > 0:
        drawn = block_levels(stream_key, extent, cuts, -0.22, 0.18) * drawn
    return jnp.clip(drawn, min=-most, max=most).astype(held_as)


def setup_inputs(seed: int = 0) -> dict:
    streams_of = jax.random.split(jax.random.key(seed), 6)
    delays = scatter_about(streams_of[0], (NROWS,), 1.0, 6.0, ((0, 32),), jnp.float32)
    kernel_tiles = scatter_about(streams_of[1], (DATA_GROUPS, MODEL_GROUPS, KT, TILE, TILE), (32 * TILE) ** -0.5, 0.09375, ((0, 32), (1, 4)))
    row_blocks = plant(jax.random.randint(streams_of[2], (DATA_GROUPS, MODEL_GROUPS, KT), 0, RB_DEV), jax.random.fold_in(streams_of[2], 1), 0, RB_DEV - 1).astype(jnp.int32)
    col_blocks = plant(jax.random.randint(streams_of[3], (DATA_GROUPS, MODEL_GROUPS, KT), 0, CB_DEV), jax.random.fold_in(streams_of[3], 1), 0, CB_DEV - 1).astype(jnp.int32)
    tile_counts = draw_tile_counts(jax.random.fold_in(streams_of[5], 71), 0)
    return {"delays": delays, "kernel_tiles": kernel_tiles, "row_blocks": row_blocks, "col_blocks": col_blocks, "tile_counts": tile_counts}


norm_eps = 1e-06

def apply_forward(kernel_tiles, row_blocks, col_blocks, tile_counts, right_raw):
    right_low = right_raw.astype(jnp.bfloat16).astype(jnp.float32).reshape(MODEL_GROUPS, CB_DEV, TILE)
    slots = jnp.arange(KT, dtype=jnp.int32)

    def one_group(pieces):
        tiles_here, rows_here, cols_here, counts_here = pieces
        picked = jax.vmap(lambda values_in, positions: values_in[positions])(right_low, cols_here)
        live = (slots[None, :] < counts_here[:, None]).astype(jnp.float32)
        products = jnp.einsum('mkij,mkj->mki', tiles_here.astype(jnp.float32), picked, precision=lax.Precision.HIGHEST) * live[:, :, None]
        return jax.ops.segment_sum(products.reshape(-1, TILE), rows_here.reshape(-1), num_segments=RB_DEV)
    return lax.map(one_group, (kernel_tiles, row_blocks, col_blocks, tile_counts)).reshape(-1)

def apply_backward(kernel_tiles, row_blocks, col_blocks, tile_counts, left_raw):
    left_low = left_raw.astype(jnp.bfloat16).astype(jnp.float32).reshape(DATA_GROUPS, RB_DEV, TILE)
    slots = jnp.arange(KT, dtype=jnp.int32)

    def add_group(total, pieces):
        tiles_here, rows_here, cols_here, counts_here, left_here = pieces
        picked = left_here[rows_here]
        live = (slots[None, :] < counts_here[:, None]).astype(jnp.float32)
        products = jnp.einsum('mkij,mki->mkj', tiles_here.astype(jnp.float32), picked, precision=lax.Precision.HIGHEST) * live[:, :, None]
        part_sum = jax.vmap(lambda prod_one, cols_one: jax.ops.segment_sum(prod_one, cols_one, num_segments=CB_DEV))(products, cols_here)
        return (total + part_sum, None)
    start_total = jnp.zeros((MODEL_GROUPS, CB_DEV, TILE), jnp.float32)
    total, unused = lax.scan(add_group, start_total, (kernel_tiles, row_blocks, col_blocks, tile_counts, left_low))
    return total.reshape(-1)

def reference(delays, kernel_tiles, row_blocks, col_blocks, tile_counts):
    beta_now = jnp.sqrt(jnp.sum(delays * delays) + norm_eps)
    left_dir = delays / beta_now
    right_raw = apply_backward(kernel_tiles, row_blocks, col_blocks, tile_counts, delays) / beta_now
    phi_bar = beta_now
    slowness = jnp.zeros((NCELLS,), jnp.float32)
    search_dir = slowness
    rho_now = beta_now
    cosine = beta_now
    sine_val = beta_now
    for iteration in range(ITERS):
        alpha_now = jnp.sqrt(jnp.sum(right_raw * right_raw) + norm_eps)
        right_dir = right_raw / alpha_now
        if iteration == 0:
            search_dir = right_dir
            rho_bar = alpha_now
        else:
            theta_now = sine_val * alpha_now
            rho_bar = -cosine * alpha_now
            search_dir = right_dir - theta_now / rho_now * search_dir
        image = apply_forward(kernel_tiles, row_blocks, col_blocks, tile_counts, right_raw)
        left_raw = image / alpha_now - alpha_now * left_dir
        beta_now = jnp.sqrt(jnp.sum(left_raw * left_raw) + norm_eps)
        left_dir = left_raw / beta_now
        rho_now = jnp.sqrt(rho_bar * rho_bar + beta_now * beta_now)
        cosine = rho_bar / rho_now
        sine_val = beta_now / rho_now
        phi_now = cosine * phi_bar
        phi_bar = sine_val * phi_bar
        slowness = slowness + phi_now / rho_now * search_dir
        if iteration + 1 < ITERS:
            back_sum = apply_backward(kernel_tiles, row_blocks, col_blocks, tile_counts, left_raw)
            right_raw = back_sum / beta_now - beta_now * right_dir
    return (slowness, left_dir)
```

```python
import jax
import jax.numpy as jnp
from jax import lax
from jax.experimental import pallas as pl
from jax.experimental.pallas import tpu as pltpu
from jax.sharding import PartitionSpec as P

TILE = 128
SLOTS = 256
HALF = SLOTS // 2
ROW_BLOCKS = 64
CELL_BLOCKS = 4096
CHUNK = CELL_BLOCKS // 32
PAIR_ROWS = SLOTS + CHUNK
BLOCK_ROWS = HALF + 8
GROUP = 8
LOAD_CHUNKS = 8
norm_eps = 1e-06

MESH = pl.DeviceIdType.MESH
F32 = jnp.float32
BF16 = jnp.bfloat16
NT = (((1,), (1,)), ((), ()))

SIDES = (1, 3, 2)


def split_parts(values):
    high = values.astype(BF16)
    low = (values - high.astype(F32)).astype(BF16)
    return high, low


def side_by_side(values):
    return jnp.concatenate(split_parts(values), axis=1)


def total_of(values):
    return jnp.sum(jnp.sum(values, axis=0, keepdims=True), axis=1, keepdims=True)


def tree4(parts):
    return (parts[0] + parts[2]) + (parts[1] + parts[3])


def lsqr_kernel(
    count_ref,
    delays_ref,
    rows_ref,
    cols_ref,
    tiles_hbm,
    slow_hbm,
    left_ref,
    tiles,
    picked,
    slot_products,
    gather_first,
    gather_second,
    targets,
    row_pick,
    row_sum,
    summed,
    cols_out,
    cols_in,
    pair_out,
    pair_in,
    image_out,
    image_in,
    norm_out,
    norm_in,
    dense_first,
    dense_second,
    slow_buf,
    load_sem,
    store_sem,
    gather_send,
    gather_recv,
    cols_sem,
    pair_sem,
    image_send,
    image_recv,
    norm_send,
    norm_recv,
    dense_send,
    dense_recv,
):
    dp = lax.axis_index("dp")
    mp = lax.axis_index("mp")
    at_x, at_z, core = dp // 8, (dp // 2) % 4, dp % 2

    def peer(off_x, off_z, off_core=0, off_y=0):
        there = ((at_x + off_x) % 4) * 8 + ((at_z + off_z) % 4) * 2 + (core + off_core) % 2
        return (there, (mp + off_y) % 4)

    sibling = peer(0, 0, 1)

    def remote(src, dst, send, recv, device):
        return pltpu.make_async_remote_copy(
            src_ref=src, dst_ref=dst, send_sem=send, recv_sem=recv, device_id=device, device_id_type=MESH
        )

    loads = []
    load_rows = SLOTS * TILE // LOAD_CHUNKS
    for part in range(LOAD_CHUNKS):
        span = pl.ds(part * load_rows, load_rows)
        load = pltpu.make_async_copy(tiles_hbm.at[span], tiles.at[span], load_sem.at[part])
        load.start()
        loads.append(load)

    barrier = pltpu.get_barrier_semaphore()
    partners = [peer(side, 0) for side in SIDES] + [peer(0, side) for side in SIDES]
    partners += [sibling] + [peer(0, 0, 0, side) for side in SIDES]
    for partner in partners:
        pl.semaphore_signal(barrier, inc=1, device_id=partner, device_id_type=MESH)

    sent = []

    count = count_ref[0, 0]
    rows_f = rows_ref[...].astype(F32)
    cols_f = cols_ref[...].astype(F32)
    lane_f = lax.broadcasted_iota(jnp.int32, (TILE, TILE), 1).astype(F32)
    sub_i = lax.broadcasted_iota(jnp.int32, (TILE, TILE), 0)
    for half in range(2):
        down = jnp.transpose(jnp.broadcast_to(rows_f[half : half + 1, :], (TILE, TILE)))
        live = sub_i + half * HALF < count
        row_pick[pl.ds(half * HALF, HALF), :] = jnp.where((down == lane_f) & live, 1.0, 0.0).astype(BF16)
        across = jnp.broadcast_to(rows_f[half : half + 1, :], (ROW_BLOCKS, TILE))
        sub_r = lax.broadcasted_iota(jnp.int32, (ROW_BLOCKS, TILE), 0).astype(F32)
        lane_r = lax.broadcasted_iota(jnp.int32, (ROW_BLOCKS, TILE), 1) + half * HALF
        row_sum[:, pl.ds(half * HALF, HALF)] = jnp.where((across == sub_r) & (lane_r < count), 1.0, 0.0).astype(BF16)
        targets[pl.ds(half * HALF, HALF), :] = jnp.transpose(
            jnp.broadcast_to(cols_f[half : half + 1, :], (TILE, TILE))
        )
    first_block = ((dp // 2) * (2 * CHUNK)).astype(F32)
    core_f = core.astype(F32)
    chunk_f = sub_i.astype(F32) + first_block
    targets[pl.ds(SLOTS, CHUNK), :] = chunk_f + core_f * CHUNK
    targets[pl.ds(PAIR_ROWS + SLOTS, CHUNK), :] = chunk_f + (1.0 - core_f) * CHUNK
    cols_out[...] = jnp.concatenate([cols_f, jnp.zeros((6, TILE), F32)], axis=0)

    def pick_rows(vector):
        padded = jnp.concatenate([vector, jnp.zeros((TILE - ROW_BLOCKS, TILE), F32)], axis=0)
        picked[...] = jnp.dot(row_pick[...], side_by_side(padded), preferred_element_type=F32)

    row_in_group = lax.broadcasted_iota(jnp.int32, (2 * GROUP, TILE), 0) % GROUP
    sub_group = lax.broadcasted_iota(jnp.int32, (GROUP, TILE), 0)

    def both_parts(group):
        span = pl.ds(group * GROUP, GROUP)
        return jnp.concatenate([picked[span, pl.ds(0, TILE)], picked[span, pl.ds(TILE, TILE)]], axis=0)

    def back_group(group, block, first):
        parts = both_parts(group)
        lhs = jnp.concatenate(
            [jnp.where(row_in_group == slot, parts, 0.0).astype(BF16) for slot in range(GROUP)], axis=1
        )
        weights = tiles[pl.ds(group * (GROUP * TILE), GROUP * TILE), :]
        out = jnp.dot(lhs, weights, preferred_element_type=F32)
        block[pl.ds((group - first) * GROUP, GROUP), :] = out[:GROUP] + out[GROUP:]

    def forward_group(group):
        lhs = both_parts(group).astype(BF16)
        weights = tiles[pl.ds(group * (GROUP * TILE), GROUP * TILE), :]
        out = lax.dot_general(lhs, weights, NT, preferred_element_type=F32)
        out = out[:GROUP] + out[GROUP:]
        chosen = out[:, :TILE]
        for slot in range(1, GROUP):
            chosen = jnp.where(sub_group == slot, out[:, slot * TILE : (slot + 1) * TILE], chosen)
        slot_products[pl.ds(group * GROUP, GROUP), :] = chosen

    def forward(right):
        high, low = split_parts(right)
        picked[:, pl.ds(0, TILE)] = high.astype(F32)
        picked[:, pl.ds(TILE, TILE)] = low.astype(F32)

        @pl.loop(0, SLOTS // GROUP, unroll=4)
        def _(group):
            forward_group(group)

        out = jnp.dot(row_sum[...], side_by_side(slot_products[...]), preferred_element_type=F32)
        return out[:, :TILE] + out[:, TILE:]

    def scalar_rows(scalars):
        rows = [jnp.broadcast_to(value, (1, TILE)) for value in scalars]
        rows = [jnp.zeros((1, TILE), F32)] + rows
        rows += [jnp.zeros((8 - len(rows), TILE), F32)]
        return jnp.concatenate(rows, axis=0)

    def back_and_gather(step, gathered, scalars, waits):
        def arrival(half, off_x, off_z):
            block = gathered.at[half, off_x, off_z]
            return remote(
                block, block, gather_send.at[step, half, off_x, off_z], gather_recv.at[step, half, off_x, off_z], sibling
            )

        def send(half, off_x, off_z, side, along_x):
            to_x, to_z = (off_x - side) % 4, (off_z - side) % 4
            dst = (to_x, off_z) if along_x else (off_x, to_z)
            device = peer(side, 0) if along_x else peer(0, side)
            copy = remote(
                gathered.at[half, off_x, off_z],
                gathered.at[half, dst[0], dst[1]],
                gather_send.at[step, half, dst[0], dst[1]],
                gather_recv.at[step, half, dst[0], dst[1]],
                device,
            )
            copy.start()
            sent.append(copy)

        chunks = LOAD_CHUNKS // 2
        groups = HALF // GROUP
        for half in range(2):
            tail = scalar_rows(scalars)
            lane_cols = jnp.broadcast_to(cols_f[half : half + 1, :], (8, TILE))
            own = gathered.at[half, 0, 0]
            own[pl.ds(HALF, 8), :] = jnp.where(sub_group == 0, lane_cols, tail)
            for part in range(chunks):
                if waits:
                    loads[half * chunks + part].wait()
                per = groups // chunks
                start = half * groups + part * per

                @pl.loop(0, per, unroll=per)
                def _(index):
                    back_group(start + index, own, half * groups)

            if waits and half == 0:
                pl.semaphore_wait(barrier, len(partners))
                swap = remote(cols_out, cols_in, cols_sem.at[0], cols_sem.at[1], sibling)
                swap.start()
                sent.append(swap)
            for side in SIDES:
                send(half, 0, 0, side, half == 0)
        for half in range(2):
            for side in SIDES:
                send(half, 0, 0, side, half == 1)
        if waits:
            swap.wait_recv()
            other = cols_in[...]
            for half in range(2):
                targets[pl.ds(PAIR_ROWS + half * HALF, HALF), :] = jnp.transpose(
                    jnp.broadcast_to(other[half : half + 1, :], (TILE, TILE))
                )
        for off in (3, 1, 2):
            arrival(0, off, 0).wait_recv()
            for side in SIDES:
                send(0, off, 0, side, False)
            arrival(1, 0, off).wait_recv()
            for side in SIDES:
                send(1, 0, off, side, True)

        order = [(0, 0)] + [(off, 0) for off in (3, 1, 2)] + [(0, off) for off in (3, 1, 2)]
        order += [(off_x, off_z) for off_z in (3, 1, 2) for off_x in (3, 1, 2)]
        for number, (off_x, off_z) in enumerate(order):
            if off_z:
                if off_x or not off_x:
                    pass
            if off_z != 0:
                arrival(0, off_x, off_z).wait_recv()
            if off_x != 0:
                arrival(1, off_x, off_z).wait_recv()
            values = jnp.concatenate(
                [
                    side_by_side(gathered[0, off_x, off_z, pl.ds(0, HALF), :]),
                    side_by_side(gathered[1, off_x, off_z, pl.ds(0, HALF), :]),
                ],
                axis=0,
            )
            ids = [gathered[half, off_x, off_z, pl.ds(HALF, 1), :] for half in range(2)]

            @pl.loop(0, 2 * PAIR_ROWS // 256)
            def _(part):
                span = pl.ds(part * 256, 256)
                want = targets[span, :]
                hits = jnp.concatenate([jnp.where(want == one, 1.0, 0.0).astype(BF16) for one in ids], axis=1)
                out = jnp.dot(hits, values, preferred_element_type=F32)
                if number == 0:
                    summed[span, :] = out
                else:
                    summed[span, :] = summed[span, :] + out

        scalar_tree = tree4(
            [tree4([gathered[0, off_x, off_z, pl.ds(HALF, 8), :] for off_x in range(4)]) for off_z in range(4)]
        )
        other_half = summed[pl.ds(PAIR_ROWS, PAIR_ROWS), :]
        pair_out[step, pl.ds(0, PAIR_ROWS), :] = other_half[:, :TILE] + other_half[:, TILE:]
        pair_out[step, pl.ds(PAIR_ROWS, 8), :] = scalar_tree
        swap_sums = remote(
            pair_out.at[step], pair_in.at[step], pair_sem.at[step, 0], pair_sem.at[step, 1], sibling
        )
        swap_sums.start()
        sent.append(swap_sums)
        mine = summed[pl.ds(0, PAIR_ROWS), :]
        mine = mine[:, :TILE] + mine[:, TILE:]
        swap_sums.wait_recv()
        mine = mine + pair_in[step, pl.ds(0, PAIR_ROWS), :]
        sums = scalar_tree + pair_in[step, pl.ds(PAIR_ROWS, 8), :]
        return mine, sums

    def dense_one(step, dense, chunk):
        dense[at_x, at_z, core] = chunk
        for along in range(2):
            for side in SIDES:
                span = pl.ds(along * (CHUNK // 2), CHUNK // 2)
                block = dense.at[at_x, at_z, core, span]
                slot = (step, 0, along, (-side) % 4)
                device = peer(0, side) if along else peer(side, 0)
                copy = remote(block, block, dense_send.at[slot], dense_recv.at[slot], device)
                copy.start()
                sent.append(copy)

    def dense_two(step, dense):
        for along in range(2):
            span = pl.ds(along * (CHUNK // 2), CHUNK // 2)
            for off in (3, 1, 2):
                if along:
                    block = dense.at[at_x, (at_z + off) % 4, core, span]
                else:
                    block = dense.at[(at_x + off) % 4, at_z, core, span]
                remote(
                    block, block, dense_send.at[step, 0, along, off], dense_recv.at[step, 0, along, off], sibling
                ).wait_recv()
        for along in range(2):
            span = pl.ds(along * (CHUNK // 2), CHUNK // 2)
            for side in SIDES:
                block = dense.at[at_x, :, core, span] if along else dense.at[:, at_z, core, span]
                device = peer(side, 0) if along else peer(0, side)
                slot = (step, 1, along, (-side) % 4)
                copy = remote(block, block, dense_send.at[slot], dense_recv.at[slot], device)
                copy.start()
                sent.append(copy)

    def dense_three(step, dense):
        for along in range(2):
            span = pl.ds(along * (CHUNK // 2), CHUNK // 2)
            for off in (3, 1, 2):
                block = (
                    dense.at[(at_x + off) % 4, :, core, span] if along else dense.at[:, (at_z + off) % 4, core, span]
                )
                remote(
                    block, block, dense_send.at[step, 1, along, off], dense_recv.at[step, 1, along, off], sibling
                ).wait_recv()
        block = dense.at[:, :, core]
        copy = remote(block, block, dense_send.at[step, 2, 0, 0], dense_recv.at[step, 2, 0, 0], sibling)
        copy.start()
        sent.append(copy)

    def dense_done(step, dense):
        block = dense.at[:, :, 1 - core]
        remote(block, block, dense_send.at[step, 2, 0, 0], dense_recv.at[step, 2, 0, 0], sibling).wait_recv()

    def image_start(step, image, scalars):
        image_out[step, pl.ds(0, ROW_BLOCKS), :] = image
        image_out[step, pl.ds(ROW_BLOCKS, 8), :] = scalar_rows(scalars)
        for side in SIDES:
            back = (-side) % 4
            copy = remote(
                image_out.at[step],
                image_in.at[step, back],
                image_send.at[step, back],
                image_recv.at[step, back],
                peer(0, 0, 0, side),
            )
            copy.start()
            sent.append(copy)

    def image_finish(step):
        for off in (3, 1, 2):
            block = image_in.at[step, off]
            remote(block, block, image_send.at[step, off], image_recv.at[step, off], sibling).wait_recv()
        parts = [image_out[step]] + [image_in[step, off] for off in (1, 2, 3)]
        total = tree4(parts)
        return total[:ROW_BLOCKS], total[ROW_BLOCKS:]

    def norm_sum(scalars):
        value = scalar_rows(scalars)
        for axis in range(2):
            norm_out[axis] = value
            for side in SIDES:
                back = (-side) % 4
                device = peer(0, side) if axis else peer(side, 0)
                copy = remote(
                    norm_out.at[axis], norm_in.at[axis, back], norm_send.at[axis, back], norm_recv.at[axis, back], device
                )
                copy.start()
                sent.append(copy)
            for off in (3, 1, 2):
                block = norm_in.at[axis, off]
                remote(block, block, norm_send.at[axis, off], norm_recv.at[axis, off], sibling).wait_recv()
            value = tree4([value] + [norm_in[axis, off] for off in (1, 2, 3)])
        norm_out[2] = value
        copy = remote(norm_out.at[2], norm_in.at[2, 0], norm_send.at[2, 0], norm_recv.at[2, 0], sibling)
        copy.start()
        sent.append(copy)
        copy.wait_recv()
        return value + norm_in[2, 0]

    def root(square):
        return jnp.sqrt(jnp.maximum(square, 0.0) + norm_eps)

    delays = delays_ref[...]
    pick_rows(delays)
    sums, scalars = back_and_gather(0, gather_first, [total_of(delays * delays)], True)
    beta_first = root(scalars[1:2])
    right_first = sums / beta_first
    right_slots, right_chunk = right_first[:SLOTS], right_first[SLOTS:]
    dense_one(0, dense_first, right_chunk)
    left_first = delays / beta_first

    image = forward(right_slots)
    image_start(0, image, [total_of(right_chunk * right_chunk)])
    dense_two(0, dense_first)
    image, scalars = image_finish(0)
    alpha_part = scalars[1:2, 0:1]

    pick_rows(image)
    scalars = [alpha_part, total_of(image * image), total_of(image * left_first), total_of(left_first * left_first)]
    dense_three(0, dense_first)
    sums, scalars = back_and_gather(1, gather_second, scalars, False)
    alpha_first = root(scalars[1:2])
    beta_second = root(
        scalars[2:3] / (alpha_first * alpha_first) - 2.0 * scalars[3:4] + alpha_first * alpha_first * scalars[4:5]
    )
    left_second = (image / alpha_first - alpha_first * left_first) / beta_second
    right_second = (sums / alpha_first - alpha_first * right_first) / beta_second
    right_second = right_second - beta_second * (right_first / alpha_first)
    right_slots, right_chunk = right_second[:SLOTS], right_second[SLOTS:]
    dense_one(1, dense_second, right_chunk)

    image = forward(right_slots)
    image_start(1, image, [total_of(right_chunk * right_chunk)])
    dense_two(1, dense_second)
    image, scalars = image_finish(1)
    alpha_part = scalars[1:2, 0:1]
    scalars = [alpha_part, total_of(image * image), total_of(image * left_second), total_of(left_second * left_second)]
    scalars = norm_sum(scalars)
    dense_three(1, dense_second)
    alpha_second = root(scalars[1:2])
    beta_third = root(
        scalars[2:3] / (alpha_second * alpha_second) - 2.0 * scalars[3:4] + alpha_second * alpha_second * scalars[4:5]
    )
    left_ref[...] = (image / alpha_second - alpha_second * left_second) / beta_third

    rho_first = jnp.sqrt(alpha_first * alpha_first + beta_second * beta_second)
    cosine = alpha_first / rho_first
    sine = beta_second / rho_first
    step_first = cosine * beta_first / rho_first
    phi_bar = sine * beta_first
    theta = sine * alpha_second
    rho_bar = -cosine * alpha_second
    rho_second = jnp.sqrt(rho_bar * rho_bar + beta_third * beta_third)
    step_second = rho_bar / rho_second * phi_bar / rho_second
    weight_first = (step_first - step_second * (theta / rho_first)) / alpha_first
    weight_second = step_second / alpha_second

    dense_done(0, dense_first)
    dense_done(1, dense_second)
    stores = []
    for off in range(4):
        for to_z in range(4):
            slow_buf[off, to_z] = dense_first[off, to_z] * weight_first + dense_second[off, to_z] * weight_second
        store = pltpu.make_async_copy(slow_buf.at[off], slow_hbm.at[off], store_sem.at[off])
        store.start()
        stores.append(store)
    for store in stores:
        store.wait()
    for copy in sent:
        copy.wait_send()


def shards(delays, kernel_tiles, row_blocks, col_blocks, tile_counts):
    dma = pltpu.SemaphoreType.DMA
    vmem = pl.BlockSpec(memory_space=pltpu.VMEM)
    dense_shape = (4, 4, 2, CHUNK, TILE)
    slowness, left = pl.pallas_call(
        lsqr_kernel,
        out_shape=(
            jax.ShapeDtypeStruct(dense_shape, F32),
            jax.ShapeDtypeStruct((ROW_BLOCKS, TILE), F32),
        ),
        in_specs=[
            pl.BlockSpec(memory_space=pltpu.SMEM),
            vmem,
            vmem,
            vmem,
            pl.BlockSpec(memory_space=pl.ANY),
        ],
        out_specs=(pl.BlockSpec(memory_space=pl.ANY), vmem),
        scratch_shapes=[
            pltpu.VMEM((SLOTS * TILE, TILE), BF16),
            pltpu.VMEM((SLOTS, 2 * TILE), F32),
            pltpu.VMEM((SLOTS, TILE), F32),
            pltpu.VMEM((2, 4, 4, BLOCK_ROWS, TILE), F32),
            pltpu.VMEM((2, 4, 4, BLOCK_ROWS, TILE), F32),
            pltpu.VMEM((2 * PAIR_ROWS, TILE), F32),
            pltpu.VMEM((SLOTS, TILE), BF16),
            pltpu.VMEM((ROW_BLOCKS, SLOTS), BF16),
            pltpu.VMEM((2 * PAIR_ROWS, 2 * TILE), F32),
            pltpu.VMEM((8, TILE), F32),
            pltpu.VMEM((8, TILE), F32),
            pltpu.VMEM((2, PAIR_ROWS + 8, TILE), F32),
            pltpu.VMEM((2, PAIR_ROWS + 8, TILE), F32),
            pltpu.VMEM((2, ROW_BLOCKS + 8, TILE), F32),
            pltpu.VMEM((2, 4, ROW_BLOCKS + 8, TILE), F32),
            pltpu.VMEM((3, 8, TILE), F32),
            pltpu.VMEM((3, 4, 8, TILE), F32),
            pltpu.VMEM(dense_shape, F32),
            pltpu.VMEM(dense_shape, F32),
            pltpu.VMEM(dense_shape, F32),
            dma((LOAD_CHUNKS,)),
            dma((4,)),
            dma((2, 2, 4, 4)),
            dma((2, 2, 4, 4)),
            dma((2,)),
            dma((2, 2)),
            dma((2, 4)),
            dma((2, 4)),
            dma((3, 4)),
            dma((3, 4)),
            dma((2, 3, 2, 4)),
            dma((2, 3, 2, 4)),
        ],
        compiler_params=pltpu.CompilerParams(
            collective_id=0, has_side_effects=True, vmem_limit_bytes=48 * 2**20
        ),
        cost_estimate=pl.CostEstimate(flops=2 * 10**9, bytes_accessed=12 * 2**20, transcendentals=0),
    )(
        tile_counts,
        delays.reshape(ROW_BLOCKS, TILE),
        row_blocks.reshape(2, HALF),
        col_blocks.reshape(2, HALF),
        kernel_tiles.reshape(SLOTS * TILE, TILE),
    )
    return slowness.reshape(-1), left.reshape(-1)


def solution(mesh):
    in_specs = (
        P("dp"),
        P("dp", "mp", None, None, None),
        P("dp", "mp", None),
        P("dp", "mp", None),
        P("dp", "mp"),
    )
    out_specs = (P("mp"), P("dp"))
    return jax.shard_map(shards, mesh=mesh, in_specs=in_specs, out_specs=out_specs, check_vma=False)
```

```python
import jax
import jax.numpy as jnp
from jax import lax
from jax.experimental import pallas as pl
from jax.experimental.pallas import tpu as pltpu
from jax.sharding import PartitionSpec as P

TILE = 128
SLOTS = 256
HALF = SLOTS // 2
ROW_BLOCKS = 64
CELL_BLOCKS = 4096
CHUNK = CELL_BLOCKS // 32
WANTED = SLOTS + CHUNK
BLOCK_ROWS = HALF + 8
GROUP = 8
LOAD_CHUNKS = 8
norm_eps = 1e-06

MESH = pl.DeviceIdType.MESH
F32 = jnp.float32
BF16 = jnp.bfloat16
NT = (((1,), (1,)), ((), ()))

SIDES = (1, 3, 2)


def split_parts(values):
    high = values.astype(BF16)
    low = (values - high.astype(F32)).astype(BF16)
    return high, low


def side_by_side(values):
    return jnp.concatenate(split_parts(values), axis=1)


def total_of(values):
    return jnp.sum(jnp.sum(values, axis=0, keepdims=True), axis=1, keepdims=True)


def tree4(parts):
    return (parts[0] + parts[2]) + (parts[1] + parts[3])


def lsqr_kernel(
    count_ref,
    delays_hbm,
    rows_hbm,
    cols_hbm,
    tiles_hbm,
    slow_hbm,
    left_ref,
    delays_ref,
    rows_ref,
    cols_ref,
    tiles,
    picked,
    slot_products,
    gathered,
    targets,
    hits,
    rhs,
    row_pick,
    row_sum,
    cols_line,
    sums_out,
    sums_in,
    chunk_out,
    chunk_in,
    image_out,
    image_in,
    norm_out,
    norm_in,
    dense_first,
    dense_second,
    slow_buf,
    load_sem,
    small_sem,
    store_sem,
    gather_send,
    gather_recv,
    cols_send,
    cols_recv,
    sums_send,
    sums_recv,
    chunk_send,
    chunk_recv,
    image_send,
    image_recv,
    norm_send,
    norm_recv,
    dense_send,
    dense_recv,
):
    dp = lax.axis_index("dp")
    mp = lax.axis_index("mp")
    at_x, at_z, core = dp // 8, (dp // 2) % 4, dp % 2

    def peer(off_x, off_z, off_core=0, off_y=0):
        there = ((at_x + off_x) % 4) * 8 + ((at_z + off_z) % 4) * 2 + (core + off_core) % 2
        return (there, (mp + off_y) % 4)

    sibling = peer(0, 0, 1)

    def remote(src, dst, send, recv, device):
        return pltpu.make_async_remote_copy(
            src_ref=src, dst_ref=dst, send_sem=send, recv_sem=recv, device_id=device, device_id_type=MESH
        )

    smalls = []
    for number, (src, dst) in enumerate(((delays_hbm, delays_ref), (rows_hbm, rows_ref), (cols_hbm, cols_ref))):
        small = pltpu.make_async_copy(src, dst, small_sem.at[number])
        small.start()
        smalls.append(small)
    loads = []
    load_rows = SLOTS * TILE // LOAD_CHUNKS
    for part in range(LOAD_CHUNKS):
        span = pl.ds(part * load_rows, load_rows)
        load = pltpu.make_async_copy(tiles_hbm.at[span], tiles.at[span], load_sem.at[part])
        load.start()
        loads.append(load)

    barrier = pltpu.get_barrier_semaphore()
    partners = [peer(side, 0) for side in SIDES] + [peer(0, side) for side in SIDES]
    partners += [sibling] + [peer(0, 0, 0, side) for side in SIDES]
    for partner in partners:
        pl.semaphore_signal(barrier, inc=1, device_id=partner, device_id_type=MESH)

    sent = []

    low_lanes = lax.broadcasted_iota(jnp.int32, (TILE, TILE), 1) < TILE // 2
    lane_f = lax.broadcasted_iota(jnp.int32, (TILE, TILE), 1).astype(F32)
    sub_i = lax.broadcasted_iota(jnp.int32, (TILE, TILE), 0)

    def lane_swap(first, second):
        low = low_lanes[: first.shape[0]]
        return (
            jnp.where(low, first, pltpu.roll(second, TILE // 2, 1)),
            jnp.where(low, pltpu.roll(first, TILE // 2, 1), second),
        )

    for small in smalls:
        small.wait()
    count = count_ref[0, 0]
    rows_f = rows_ref[...].astype(F32)
    cols_f = cols_ref[...].astype(F32)
    for half in range(2):
        down = jnp.transpose(jnp.broadcast_to(rows_f[half : half + 1, :], (TILE, TILE)))
        live = sub_i + half * HALF < count
        row_pick[pl.ds(half * HALF, HALF), :] = jnp.where((down == lane_f) & live, 1.0, 0.0).astype(BF16)
        across = jnp.broadcast_to(rows_f[half : half + 1, :], (ROW_BLOCKS, TILE))
        sub_r = lax.broadcasted_iota(jnp.int32, (ROW_BLOCKS, TILE), 0).astype(F32)
        lane_r = lax.broadcasted_iota(jnp.int32, (ROW_BLOCKS, TILE), 1) + half * HALF
        row_sum[:, pl.ds(half * HALF, HALF)] = jnp.where((across == sub_r) & (lane_r < count), 1.0, 0.0).astype(BF16)
    own_cols = jnp.concatenate([cols_f, jnp.zeros((6, TILE), F32)], axis=0)
    for axis in range(2):
        cols_line[axis, 0, 0] = own_cols

    def target_rows(axis, off):
        start = off * WANTED
        for half in range(2):
            targets[axis, pl.ds(start + half * HALF, HALF), :] = jnp.transpose(
                jnp.broadcast_to(cols_line[1 - axis, 0, off, pl.ds(half, 1), :], (TILE, TILE))
            )
        device = peer(off, 0)[0] if axis else peer(0, off)[0]
        targets[axis, pl.ds(start + SLOTS, CHUNK), :] = (sub_i + device * CHUNK).astype(F32)

    def pick_rows(vector):
        padded = jnp.concatenate([vector, jnp.zeros((TILE - ROW_BLOCKS, TILE), F32)], axis=0)
        picked[...] = jnp.dot(row_pick[...], side_by_side(padded), preferred_element_type=F32)

    row_in_group = lax.broadcasted_iota(jnp.int32, (2 * GROUP, TILE), 0) % GROUP
    sub_group = lax.broadcasted_iota(jnp.int32, (GROUP, TILE), 0)

    def both_parts(group):
        span = pl.ds(group * GROUP, GROUP)
        return jnp.concatenate([picked[span, pl.ds(0, TILE)], picked[span, pl.ds(TILE, TILE)]], axis=0)

    def back_group(group):
        parts = both_parts(group)
        lhs = jnp.concatenate(
            [jnp.where(row_in_group == slot, parts, 0.0).astype(BF16) for slot in range(GROUP)], axis=1
        )
        weights = tiles[pl.ds(group * (GROUP * TILE), GROUP * TILE), :]
        out = jnp.dot(lhs, weights, preferred_element_type=F32)
        return out[:GROUP] + out[GROUP:]

    def forward_group(group):
        lhs = both_parts(group).astype(BF16)
        weights = tiles[pl.ds(group * (GROUP * TILE), GROUP * TILE), :]
        out = lax.dot_general(lhs, weights, NT, preferred_element_type=F32)
        out = out[:GROUP] + out[GROUP:]
        chosen = out[:, :TILE]
        for slot in range(1, GROUP):
            chosen = jnp.where(sub_group == slot, out[:, slot * TILE : (slot + 1) * TILE], chosen)
        slot_products[pl.ds(group * GROUP, GROUP), :] = chosen

    def forward(right, between):
        high, low = split_parts(right)
        picked[:, pl.ds(0, TILE)] = high.astype(F32)
        picked[:, pl.ds(TILE, TILE)] = low.astype(F32)
        half = SLOTS // GROUP // 2

        @pl.loop(0, half, unroll=4)
        def _(group):
            forward_group(group)

        result = between()

        @pl.loop(half, 2 * half, unroll=4)
        def _(group):
            forward_group(group)

        out = jnp.dot(row_sum[...], side_by_side(slot_products[...]), preferred_element_type=F32)
        return out[:, :TILE] + out[:, TILE:], result

    def scalar_rows(scalars):
        rows = [jnp.broadcast_to(value, (1, TILE)) for value in scalars]
        rows += [jnp.zeros((8 - len(rows), TILE), F32)]
        return jnp.concatenate(rows, axis=0)

    def line(axis, off, core_off=0):
        return peer(0, off, core_off) if axis else peer(off, 0, core_off)

    def exchange_cols():
        copies = []
        for axis in range(2):
            for side in SIDES:
                back = (-side) % 4
                copy = remote(
                    cols_line.at[axis, 0, 0],
                    cols_line.at[axis, 0, back],
                    cols_send.at[axis, 0, back],
                    cols_recv.at[axis, 0, back],
                    line(axis, side),
                )
                copy.start()
                copies.append(copy)
        sent.extend(copies)
        return copies

    def spread_cols(copies):
        for axis in range(2):
            target_rows(axis, 0)
        for copy in copies:
            copy.wait_recv()
        across = []
        for axis in range(2):
            copy = remote(
                cols_line.at[axis, 0], cols_line.at[axis, 1], cols_send.at[axis, 1, 0], cols_recv.at[axis, 1, 0], sibling
            )
            copy.start()
            across.append(copy)
        sent.extend(across)
        for axis in range(2):
            for off in (1, 2, 3):
                target_rows(axis, off)
        for copy in across:
            copy.wait_recv()
        for axis in range(2):

            @pl.loop(0, 4 * WANTED // TILE)
            def _(part):
                span = pl.ds(part * TILE, TILE)
                want = targets[axis, span, :]
                for off in range(4):
                    for core_off in range(2):
                        for half in range(2):
                            one = cols_line[axis, core_off, off, pl.ds(half, 1), :]
                            column = ((off * 2 + core_off) * 2 + half) * HALF
                            hits[axis, span, pl.ds(column, HALF)] = jnp.where(want == one, 1.0, 0.0).astype(BF16)

    def back_and_gather(step, scalars, first_step):
        def arrival(axis, core_off, off):
            block = gathered.at[step, axis, core_off, off]
            slot = (step, axis, core_off, off)
            return remote(block, block, gather_send.at[slot], gather_recv.at[slot], sibling)

        tail = scalar_rows(scalars)
        for axis in range(2):
            gathered[step, axis, 0, 0, pl.ds(HALF, 8), :] = tail
        chunks = LOAD_CHUNKS // 2
        groups = HALF // GROUP
        per = groups // chunks
        for part in range(chunks):
            if first_step:
                loads[part].wait()
                loads[chunks + part].wait()

            @pl.loop(0, per, unroll=per)
            def _(index):
                group = part * per + index
                low, high = lane_swap(back_group(group), back_group(groups + group))
                span = pl.ds(group * GROUP, GROUP)
                gathered[step, 0, 0, 0, span, :] = low
                gathered[step, 1, 0, 0, span, :] = high

        if first_step:
            pl.semaphore_wait(barrier, len(partners))
            cols_copies = exchange_cols()

        def send(axis, core_off, off, to_core, to_off, device):
            slot = (step, axis, to_core, to_off)
            copy = remote(
                gathered.at[step, axis, core_off, off],
                gathered.at[slot],
                gather_send.at[slot],
                gather_recv.at[slot],
                device,
            )
            copy.start()
            sent.append(copy)

        for side in SIDES:
            for axis in range(2):
                send(axis, 0, 0, 0, (-side) % 4, line(axis, side))
        for axis in range(2):
            send(axis, 0, 0, 1, 0, sibling)
        if first_step:
            spread_cols(cols_copies)
        for off in (3, 1, 2):
            for axis in range(2):
                arrival(axis, 0, off).wait_recv()
                send(axis, 0, off, 1, off, sibling)

        def take(axis, core_off, off):
            block = gathered[step, axis, core_off, off, pl.ds(0, HALF), :]
            high = block.astype(BF16).astype(F32)
            first, second = lane_swap(high, block - high)
            row = (off * 2 + core_off) * SLOTS
            rhs[axis, pl.ds(row, HALF), :] = first.astype(BF16)
            rhs[axis, pl.ds(row + HALF, HALF), :] = second.astype(BF16)

        for axis in range(2):
            for off in range(4):
                take(axis, 0, off)
        for axis in range(2):
            for off in (0, 3, 1, 2):
                arrival(axis, 1, off).wait_recv()
                take(axis, 1, off)

        line_scalars = tree4([gathered[step, 0, 0, off, pl.ds(HALF, 8), :] for off in range(4)])
        line_scalars = line_scalars + tree4([gathered[step, 0, 1, off, pl.ds(HALF, 8), :] for off in range(4)])

        def wanted_sums(axis, off, start, size):
            out = jnp.dot(
                hits[axis, pl.ds(off * WANTED + start, size), :], rhs[axis], preferred_element_type=F32
            )
            out = out + pltpu.roll(out, TILE // 2, 1)
            return jnp.where(low_lanes[: size // 2], out[: size // 2], out[size // 2 :])

        for axis in range(2):
            for off in SIDES + (0,):
                sums_out[step, axis, off, pl.ds(0, HALF), :] = wanted_sums(axis, off, 0, SLOTS)
                sums_out[step, axis, off, pl.ds(HALF, 8), :] = line_scalars
                if off:
                    slot = (step, axis, (-off) % 4)
                    copy = remote(
                        sums_out.at[step, axis, off],
                        sums_in.at[slot],
                        sums_send.at[slot],
                        sums_recv.at[slot],
                        line(1 - axis, off),
                    )
                    copy.start()
                    sent.append(copy)
        for axis in range(2):
            for off in SIDES + (0,):
                chunk_out[step, axis, off] = wanted_sums(axis, off, SLOTS, CHUNK)
                if off:
                    slot = (step, axis, (-off) % 4)
                    copy = remote(
                        chunk_out.at[step, axis, off],
                        chunk_in.at[slot],
                        chunk_send.at[slot],
                        chunk_recv.at[slot],
                        line(1 - axis, off),
                    )
                    copy.start()
                    sent.append(copy)
        totals = []
        for axis in range(2):
            for off in (3, 1, 2):
                block = sums_in.at[step, axis, off]
                slot = (step, axis, off)
                remote(block, block, sums_send.at[slot], sums_recv.at[slot], sibling).wait_recv()
            totals.append(tree4([sums_out[step, axis, 0]] + [sums_in[step, axis, off] for off in (1, 2, 3)]))
        mine = jnp.concatenate(lane_swap(totals[0][:HALF], totals[1][:HALF]), axis=0)
        return mine, totals[0][HALF:]

    def chunk_sums(step):
        totals = []
        for axis in range(2):
            for off in (3, 1, 2):
                block = chunk_in.at[step, axis, off]
                slot = (step, axis, off)
                remote(block, block, chunk_send.at[slot], chunk_recv.at[slot], sibling).wait_recv()
            totals.append(tree4([chunk_out[step, axis, 0]] + [chunk_in[step, axis, off] for off in (1, 2, 3)]))
        return jnp.concatenate(lane_swap(totals[0], totals[1]), axis=0)

    def dense_one(step, dense, chunk):
        dense[at_x, at_z, core] = chunk
        for along in range(2):
            for side in SIDES:
                span = pl.ds(along * (CHUNK // 2), CHUNK // 2)
                block = dense.at[at_x, at_z, core, span]
                slot = (step, 0, along, (-side) % 4)
                device = peer(0, side) if along else peer(side, 0)
                copy = remote(block, block, dense_send.at[slot], dense_recv.at[slot], device)
                copy.start()
                sent.append(copy)

    def dense_two(step, dense):
        for along in range(2):
            span = pl.ds(along * (CHUNK // 2), CHUNK // 2)
            for off in (3, 1, 2):
                if along:
                    block = dense.at[at_x, (at_z + off) % 4, core, span]
                else:
                    block = dense.at[(at_x + off) % 4, at_z, core, span]
                remote(
                    block, block, dense_send.at[step, 0, along, off], dense_recv.at[step, 0, along, off], sibling
                ).wait_recv()
        for along in range(2):
            span = pl.ds(along * (CHUNK // 2), CHUNK // 2)
            for side in SIDES:
                block = dense.at[at_x, :, core, span] if along else dense.at[:, at_z, core, span]
                device = peer(side, 0) if along else peer(0, side)
                slot = (step, 1, along, (-side) % 4)
                copy = remote(block, block, dense_send.at[slot], dense_recv.at[slot], device)
                copy.start()
                sent.append(copy)

    def dense_three(step, dense):
        for along in range(2):
            span = pl.ds(along * (CHUNK // 2), CHUNK // 2)
            for off in (3, 1, 2):
                block = (
                    dense.at[(at_x + off) % 4, :, core, span] if along else dense.at[:, (at_z + off) % 4, core, span]
                )
                remote(
                    block, block, dense_send.at[step, 1, along, off], dense_recv.at[step, 1, along, off], sibling
                ).wait_recv()
        block = dense.at[:, :, core]
        copy = remote(block, block, dense_send.at[step, 2, 0, 0], dense_recv.at[step, 2, 0, 0], sibling)
        copy.start()
        sent.append(copy)

    def dense_done(step, dense):
        block = dense.at[:, :, 1 - core]
        remote(block, block, dense_send.at[step, 2, 0, 0], dense_recv.at[step, 2, 0, 0], sibling).wait_recv()

    def image_start(step, image, scalars):
        image_out[step, pl.ds(0, ROW_BLOCKS), :] = image
        image_out[step, pl.ds(ROW_BLOCKS, 8), :] = scalar_rows(scalars)
        for side in SIDES:
            back = (-side) % 4
            copy = remote(
                image_out.at[step],
                image_in.at[step, back],
                image_send.at[step, back],
                image_recv.at[step, back],
                peer(0, 0, 0, side),
            )
            copy.start()
            sent.append(copy)

    def image_finish(step):
        for off in (3, 1, 2):
            block = image_in.at[step, off]
            remote(block, block, image_send.at[step, off], image_recv.at[step, off], sibling).wait_recv()
        parts = [image_out[step]] + [image_in[step, off] for off in (1, 2, 3)]
        total = tree4(parts)
        return total[:ROW_BLOCKS], total[ROW_BLOCKS:]

    def norm_sum(scalars):
        value = scalar_rows(scalars)
        for axis in range(2):
            norm_out[axis] = value
            for side in SIDES:
                back = (-side) % 4
                device = peer(0, side) if axis else peer(side, 0)
                copy = remote(
                    norm_out.at[axis], norm_in.at[axis, back], norm_send.at[axis, back], norm_recv.at[axis, back], device
                )
                copy.start()
                sent.append(copy)
            for off in (3, 1, 2):
                block = norm_in.at[axis, off]
                remote(block, block, norm_send.at[axis, off], norm_recv.at[axis, off], sibling).wait_recv()
            value = tree4([value] + [norm_in[axis, off] for off in (1, 2, 3)])
        norm_out[2] = value
        copy = remote(norm_out.at[2], norm_in.at[2, 0], norm_send.at[2, 0], norm_recv.at[2, 0], sibling)
        copy.start()
        sent.append(copy)
        copy.wait_recv()
        return value + norm_in[2, 0]

    def root(square):
        return jnp.sqrt(jnp.maximum(square, 0.0) + norm_eps)

    delays = delays_ref[...]
    pick_rows(delays)
    sums, scalars = back_and_gather(0, [total_of(delays * delays)], True)
    beta_first = root(scalars[0:1])
    right_first = sums / beta_first
    left_first = delays / beta_first

    def finish_first():
        chunk = chunk_sums(0) / beta_first
        dense_one(0, dense_first, chunk)
        return chunk

    image, chunk_first = forward(right_first, finish_first)
    image_start(0, image, [total_of(chunk_first * chunk_first)])
    dense_two(0, dense_first)
    image, scalars = image_finish(0)
    alpha_part = scalars[0:1, 0:1]

    pick_rows(image)
    scalars = [alpha_part, total_of(image * image), total_of(image * left_first), total_of(left_first * left_first)]
    dense_three(0, dense_first)
    sums, scalars = back_and_gather(1, scalars, False)
    alpha_first = root(scalars[0:1])
    beta_second = root(
        scalars[1:2] / (alpha_first * alpha_first) - 2.0 * scalars[2:3] + alpha_first * alpha_first * scalars[3:4]
    )
    left_second = (image / alpha_first - alpha_first * left_first) / beta_second

    def second_right(back, right):
        fresh = (back / alpha_first - alpha_first * right) / beta_second
        return fresh - beta_second * (right / alpha_first)

    def finish_second():
        chunk = second_right(chunk_sums(1), chunk_first)
        dense_one(1, dense_second, chunk)
        return chunk

    image, chunk_second = forward(second_right(sums, right_first), finish_second)
    image_start(1, image, [total_of(chunk_second * chunk_second)])
    dense_two(1, dense_second)
    image, scalars = image_finish(1)
    alpha_part = scalars[0:1, 0:1]
    scalars = [alpha_part, total_of(image * image), total_of(image * left_second), total_of(left_second * left_second)]
    scalars = norm_sum(scalars)
    dense_three(1, dense_second)
    alpha_second = root(scalars[0:1])
    beta_third = root(
        scalars[1:2] / (alpha_second * alpha_second) - 2.0 * scalars[2:3] + alpha_second * alpha_second * scalars[3:4]
    )
    left_ref[...] = (image / alpha_second - alpha_second * left_second) / beta_third

    rho_first = jnp.sqrt(alpha_first * alpha_first + beta_second * beta_second)
    cosine = alpha_first / rho_first
    sine = beta_second / rho_first
    step_first = cosine * beta_first / rho_first
    phi_bar = sine * beta_first
    theta = sine * alpha_second
    rho_bar = -cosine * alpha_second
    rho_second = jnp.sqrt(rho_bar * rho_bar + beta_third * beta_third)
    step_second = rho_bar / rho_second * phi_bar / rho_second
    weight_first = (step_first - step_second * (theta / rho_first)) / alpha_first
    weight_second = step_second / alpha_second

    dense_done(0, dense_first)
    dense_done(1, dense_second)
    stores = []
    for off in range(4):
        for to_z in range(4):
            slow_buf[off, to_z] = dense_first[off, to_z] * weight_first + dense_second[off, to_z] * weight_second
        store = pltpu.make_async_copy(slow_buf.at[off], slow_hbm.at[off], store_sem.at[off])
        store.start()
        stores.append(store)
    for store in stores:
        store.wait()
    for copy in sent:
        copy.wait_send()


def shards(delays, kernel_tiles, row_blocks, col_blocks, tile_counts):
    dma = pltpu.SemaphoreType.DMA
    vmem = pl.BlockSpec(memory_space=pltpu.VMEM)
    hbm = pl.BlockSpec(memory_space=pl.ANY)
    dense_shape = (4, 4, 2, CHUNK, TILE)
    slowness, left = pl.pallas_call(
        lsqr_kernel,
        out_shape=(
            jax.ShapeDtypeStruct(dense_shape, F32),
            jax.ShapeDtypeStruct((ROW_BLOCKS, TILE), F32),
        ),
        in_specs=[pl.BlockSpec(memory_space=pltpu.SMEM)] + [hbm] * 4,
        out_specs=(hbm, vmem),
        scratch_shapes=[
            pltpu.VMEM((ROW_BLOCKS, TILE), F32),
            pltpu.VMEM((2, HALF), jnp.int32),
            pltpu.VMEM((2, HALF), jnp.int32),
            pltpu.VMEM((SLOTS * TILE, TILE), BF16),
            pltpu.VMEM((SLOTS, 2 * TILE), F32),
            pltpu.VMEM((SLOTS, TILE), F32),
            pltpu.VMEM((2, 2, 2, 4, BLOCK_ROWS, TILE), F32),
            pltpu.VMEM((2, 4 * WANTED, TILE), F32),
            pltpu.VMEM((2, 4 * WANTED, 8 * SLOTS), BF16),
            pltpu.VMEM((2, 8 * SLOTS, TILE), BF16),
            pltpu.VMEM((SLOTS, TILE), BF16),
            pltpu.VMEM((ROW_BLOCKS, SLOTS), BF16),
            pltpu.VMEM((2, 2, 4, 8, TILE), F32),
            pltpu.VMEM((2, 2, 4, BLOCK_ROWS, TILE), F32),
            pltpu.VMEM((2, 2, 4, BLOCK_ROWS, TILE), F32),
            pltpu.VMEM((2, 2, 4, CHUNK // 2, TILE), F32),
            pltpu.VMEM((2, 2, 4, CHUNK // 2, TILE), F32),
            pltpu.VMEM((2, ROW_BLOCKS + 8, TILE), F32),
            pltpu.VMEM((2, 4, ROW_BLOCKS + 8, TILE), F32),
            pltpu.VMEM((3, 8, TILE), F32),
            pltpu.VMEM((3, 4, 8, TILE), F32),
            pltpu.VMEM(dense_shape, F32),
            pltpu.VMEM(dense_shape, F32),
            pltpu.VMEM(dense_shape, F32),
            dma((LOAD_CHUNKS,)),
            dma((3,)),
            dma((4,)),
            dma((2, 2, 2, 4)),
            dma((2, 2, 2, 4)),
            dma((2, 2, 4)),
            dma((2, 2, 4)),
            dma((2, 2, 4)),
            dma((2, 2, 4)),
            dma((2, 2, 4)),
            dma((2, 2, 4)),
            dma((2, 4)),
            dma((2, 4)),
            dma((3, 4)),
            dma((3, 4)),
            dma((2, 3, 2, 4)),
            dma((2, 3, 2, 4)),
        ],
        compiler_params=pltpu.CompilerParams(
            collective_id=0, has_side_effects=True, vmem_limit_bytes=48 * 2**20
        ),
        cost_estimate=pl.CostEstimate(flops=2 * 10**9, bytes_accessed=12 * 2**20, transcendentals=0),
    )(
        tile_counts,
        delays.reshape(ROW_BLOCKS, TILE),
        row_blocks.reshape(2, HALF),
        col_blocks.reshape(2, HALF),
        kernel_tiles.reshape(SLOTS * TILE, TILE),
    )
    return slowness.reshape(-1), left.reshape(-1)


def solution(mesh):
    in_specs = (
        P("dp"),
        P("dp", "mp", None, None, None),
        P("dp", "mp", None),
        P("dp", "mp", None),
        P("dp", "mp"),
    )
    out_specs = (P("mp"), P("dp"))
    return jax.shard_map(shards, mesh=mesh, in_specs=in_specs, out_specs=out_specs, check_vma=False)
```

```python
import jax
import jax.numpy as jnp
from jax import lax
from jax.experimental import pallas as pl
from jax.experimental.pallas import tpu as pltpu
from jax.sharding import PartitionSpec as P

TILE = 128
SLOTS = 256
HALF = SLOTS // 2
ROW_BLOCKS = 64
CELL_BLOCKS = 4096
CHUNK = CELL_BLOCKS // 32
BLOCK_ROWS = HALF + 8
GROUP = 8
LOAD_CHUNKS = 8
norm_eps = 1e-06

MESH = pl.DeviceIdType.MESH
F32 = jnp.float32
BF16 = jnp.bfloat16
NT = (((1,), (1,)), ((), ()))

SIDES = (2, 1, 3)


def split_parts(values):
    high = values.astype(BF16)
    low = (values - high.astype(F32)).astype(BF16)
    return high, low


def side_by_side(values):
    return jnp.concatenate(split_parts(values), axis=1)


def total_of(values):
    return jnp.sum(jnp.sum(values, axis=0, keepdims=True), axis=1, keepdims=True)


def tree4(parts):
    return (parts[0] + parts[2]) + (parts[1] + parts[3])


def lsqr_kernel(
    count_ref,
    delays_hbm,
    rows_hbm,
    cols_hbm,
    tiles_hbm,
    slow_hbm,
    left_ref,
    delays_ref,
    rows_ref,
    cols_ref,
    tiles,
    picked,
    slot_products,
    gathered,
    targets,
    slot_hits,
    chunk_hits,
    rhs,
    row_pick,
    row_sum,
    cols_line,
    sums_out,
    sums_in,
    chunk_out,
    chunk_in,
    image_out,
    image_in,
    norm_out,
    norm_in,
    dense_first,
    dense_second,
    slow_buf,
    load_sem,
    small_sem,
    store_sem,
    gather_send,
    gather_recv,
    cols_send,
    cols_recv,
    sums_send,
    sums_recv,
    chunk_send,
    chunk_recv,
    image_send,
    image_recv,
    norm_send,
    norm_recv,
    dense_send,
    dense_recv,
):
    dp = lax.axis_index("dp")
    mp = lax.axis_index("mp")
    at_x, at_z, core = dp // 8, (dp // 2) % 4, dp % 2

    def peer(off_x, off_z, off_core=0, off_y=0):
        there = ((at_x + off_x) % 4) * 8 + ((at_z + off_z) % 4) * 2 + (core + off_core) % 2
        return (there, (mp + off_y) % 4)

    sibling = peer(0, 0, 1)

    def remote(src, dst, send, recv, device):
        return pltpu.make_async_remote_copy(
            src_ref=src, dst_ref=dst, send_sem=send, recv_sem=recv, device_id=device, device_id_type=MESH
        )

    smalls = []
    for number, (src, dst) in enumerate(((delays_hbm, delays_ref), (rows_hbm, rows_ref), (cols_hbm, cols_ref))):
        small = pltpu.make_async_copy(src, dst, small_sem.at[number])
        small.start()
        smalls.append(small)
    load_rows = SLOTS * TILE // LOAD_CHUNKS
    loads = [None] * LOAD_CHUNKS
    for part in [p for q in range(LOAD_CHUNKS // 2) for p in (q, q + LOAD_CHUNKS // 2)]:
        span = pl.ds(part * load_rows, load_rows)
        load = pltpu.make_async_copy(tiles_hbm.at[span], tiles.at[span], load_sem.at[part])
        load.start()
        loads[part] = load

    barrier = pltpu.get_barrier_semaphore()
    partners = [peer(side, 0) for side in SIDES] + [peer(0, side) for side in SIDES]
    partners += [sibling] + [peer(0, 0, 0, side) for side in SIDES]
    for partner in partners:
        pl.semaphore_signal(barrier, inc=1, device_id=partner, device_id_type=MESH)

    sent = []

    low_lanes = lax.broadcasted_iota(jnp.int32, (TILE, TILE), 1) < TILE // 2
    lane_f = lax.broadcasted_iota(jnp.int32, (TILE, TILE), 1).astype(F32)
    sub_i = lax.broadcasted_iota(jnp.int32, (TILE, TILE), 0)

    def lane_swap(first, second):
        low = low_lanes[: first.shape[0]]
        return (
            jnp.where(low, first, pltpu.roll(second, TILE // 2, 1)),
            jnp.where(low, pltpu.roll(first, TILE // 2, 1), second),
        )

    for small in smalls:
        small.wait()
    count = count_ref[0, 0]
    rows_f = rows_ref[...].astype(F32)
    cols_f = cols_ref[...].astype(F32)
    for half in range(2):
        down = jnp.transpose(jnp.broadcast_to(rows_f[half : half + 1, :], (TILE, TILE)))
        live = sub_i + half * HALF < count
        row_pick[pl.ds(half * HALF, HALF), :] = jnp.where((down == lane_f) & live, 1.0, 0.0).astype(BF16)
        across = jnp.broadcast_to(rows_f[half : half + 1, :], (ROW_BLOCKS, TILE))
        sub_r = lax.broadcasted_iota(jnp.int32, (ROW_BLOCKS, TILE), 0).astype(F32)
        lane_r = lax.broadcasted_iota(jnp.int32, (ROW_BLOCKS, TILE), 1) + half * HALF
        row_sum[:, pl.ds(half * HALF, HALF)] = jnp.where((across == sub_r) & (lane_r < count), 1.0, 0.0).astype(BF16)
    own_cols = jnp.concatenate([cols_f, jnp.zeros((6, TILE), F32)], axis=0)
    for axis in range(2):
        cols_line[axis, 0, 0] = own_cols

    def slot_targets(axis):
        wanted = jnp.concatenate([cols_line[1 - axis, 0, off, pl.ds(0, 2), :] for off in range(4)], axis=0)
        down = jnp.transpose(jnp.concatenate([wanted, jnp.zeros((TILE - 8, TILE), F32)], axis=0))
        for part in range(8):
            targets[axis, pl.ds(part * HALF, HALF), :] = jnp.broadcast_to(down[:, part : part + 1], (HALF, TILE))

    def pick_rows(vector):
        padded = jnp.concatenate([vector, jnp.zeros((TILE - ROW_BLOCKS, TILE), F32)], axis=0)
        picked[...] = jnp.dot(row_pick[...], side_by_side(padded), preferred_element_type=F32)

    row_in_group = lax.broadcasted_iota(jnp.int32, (2 * GROUP, TILE), 0) % GROUP
    sub_group = lax.broadcasted_iota(jnp.int32, (GROUP, TILE), 0)

    def both_parts(group):
        span = pl.ds(group * GROUP, GROUP)
        return jnp.concatenate([picked[span, pl.ds(0, TILE)], picked[span, pl.ds(TILE, TILE)]], axis=0)

    def back_group(group):
        parts = both_parts(group)
        lhs = jnp.concatenate(
            [jnp.where(row_in_group == slot, parts, 0.0).astype(BF16) for slot in range(GROUP)], axis=1
        )
        weights = tiles[pl.ds(group * (GROUP * TILE), GROUP * TILE), :]
        out = jnp.dot(lhs, weights, preferred_element_type=F32)
        return out[:GROUP] + out[GROUP:]

    def forward_group(group):
        lhs = both_parts(group).astype(BF16)
        weights = tiles[pl.ds(group * (GROUP * TILE), GROUP * TILE), :]
        out = lax.dot_general(lhs, weights, NT, preferred_element_type=F32)
        out = out[:GROUP] + out[GROUP:]
        chosen = out[:, :TILE]
        for slot in range(1, GROUP):
            chosen = jnp.where(sub_group == slot, out[:, slot * TILE : (slot + 1) * TILE], chosen)
        slot_products[pl.ds(group * GROUP, GROUP), :] = chosen

    def forward(right, between):
        high, low = split_parts(right)
        picked[:, pl.ds(0, TILE)] = high.astype(F32)
        picked[:, pl.ds(TILE, TILE)] = low.astype(F32)
        half = SLOTS // GROUP // 2

        @pl.loop(0, half, unroll=8)
        def _(group):
            forward_group(group)

        result = between()

        @pl.loop(half, 2 * half, unroll=8)
        def _(group):
            forward_group(group)

        out = jnp.dot(row_sum[...], side_by_side(slot_products[...]), preferred_element_type=F32)
        return out[:, :TILE] + out[:, TILE:], result

    def scalar_rows(scalars):
        rows = [jnp.broadcast_to(value, (1, TILE)) for value in scalars]
        rows += [jnp.zeros((8 - len(rows), TILE), F32)]
        return jnp.concatenate(rows, axis=0)

    def line(axis, off, core_off=0):
        return peer(0, off, core_off) if axis else peer(off, 0, core_off)

    def exchange_cols():
        copies = []
        for axis in range(2):
            for side in SIDES:
                back = (-side) % 4
                copy = remote(
                    cols_line.at[axis, 0, 0],
                    cols_line.at[axis, 0, back],
                    cols_send.at[axis, 0, back],
                    cols_recv.at[axis, 0, back],
                    line(axis, side),
                )
                copy.start()
                copies.append(copy)
        sent.extend(copies)
        return copies

    def mark(dst, axis, span, want, core_off):
        for off in range(4):
            for half in range(2):
                one = cols_line[axis, core_off, off, pl.ds(half, 1), :]
                column = ((core_off * 4 + off) * 2 + half) * HALF
                dst[axis, span, pl.ds(column, HALF)] = jnp.where(want == one, 1.0, 0.0).astype(BF16)

    def mark_slots(core_off):
        for axis in range(2):

            @pl.loop(0, 4 * SLOTS // TILE)
            def _(part):
                span = pl.ds(part * TILE, TILE)
                mark(slot_hits, axis, span, targets[axis, span, :], core_off)

    def mark_chunks():
        for axis in range(2):

            @pl.loop(0, 4)
            def _(off):
                device = peer(off, 0)[0] if axis else peer(0, off)[0]
                want = (sub_i + device * CHUNK).astype(F32)
                for core_off in range(2):
                    mark(chunk_hits, axis, pl.ds(off * CHUNK, CHUNK), want, core_off)

    def spread_cols(copies):
        for copy in copies:
            copy.wait_recv()
        across = []
        for axis in range(2):
            copy = remote(
                cols_line.at[axis, 0], cols_line.at[axis, 1], cols_send.at[axis, 1, 0], cols_recv.at[axis, 1, 0], sibling
            )
            copy.start()
            across.append(copy)
        sent.extend(across)
        for axis in range(2):
            slot_targets(axis)
        mark_slots(0)
        for copy in across:
            copy.wait_recv()
        mark_slots(1)

    def back_and_gather(step, scalars, first_step):
        def arrival(axis, off, piece):
            span = (pl.ds(0, HALF // 2), pl.ds(HALF // 2, BLOCK_ROWS - HALF // 2))[piece]
            block = gathered.at[step, axis, 0, off, span]
            slot = (piece, step, axis, 0, off)
            return remote(block, block, gather_send.at[slot], gather_recv.at[slot], sibling)

        tail = scalar_rows(scalars)
        for axis in range(2):
            gathered[step, axis, 0, 0, pl.ds(HALF, 8), :] = tail
        chunks = LOAD_CHUNKS // 2
        groups = HALF // GROUP
        per = groups // chunks
        def send(axis, to_off, device, piece):
            span = (pl.ds(0, HALF // 2), pl.ds(HALF // 2, BLOCK_ROWS - HALF // 2))[piece]
            copy = remote(
                gathered.at[step, axis, 0, 0, span],
                gathered.at[step, axis, 0, to_off, span],
                gather_send.at[piece, step, axis, 0, to_off],
                gather_recv.at[piece, step, axis, 0, to_off],
                device,
            )
            copy.start()
            sent.append(copy)

        def across(axis, off):
            block = gathered.at[step, axis, 0, off]
            slot = (0, step, axis, 1, off)
            copy = remote(block, gathered.at[step, axis, 1, off], gather_send.at[slot], gather_recv.at[slot], sibling)
            copy.start()
            sent.append(copy)

        for part in range(chunks):
            if first_step:
                loads[part].wait()
                loads[chunks + part].wait()

            @pl.loop(0, per, unroll=per)
            def _(index):
                group = part * per + index
                low, high = lane_swap(back_group(group), back_group(groups + group))
                span = pl.ds(group * GROUP, GROUP)
                gathered[step, 0, 0, 0, span, :] = low
                gathered[step, 1, 0, 0, span, :] = high

            if 2 * (part + 1) % chunks == 0:
                piece = 2 * (part + 1) // chunks - 1
                if first_step and piece == 0:
                    pl.semaphore_wait(barrier, len(partners))
                    cols_copies = exchange_cols()
                for side in SIDES:
                    for axis in range(2):
                        send(axis, (-side) % 4, line(axis, side), piece)
        for axis in range(2):
            across(axis, 0)
        if first_step:
            spread_cols(cols_copies)
        for off in (3, 1, 2):
            for axis in range(2):
                for piece in range(2):
                    arrival(axis, off, piece).wait_recv()
                across(axis, off)

        def take(axis, core_off, off):
            block = gathered[step, axis, core_off, off, pl.ds(0, HALF), :]
            high = block.astype(BF16).astype(F32)
            first, second = lane_swap(high, block - high)
            row = (core_off * 4 + off) * SLOTS
            rhs[axis, pl.ds(row, HALF), :] = first.astype(BF16)
            rhs[axis, pl.ds(row + HALF, HALF), :] = second.astype(BF16)

        for axis in range(2):
            for off in range(4):
                take(axis, 0, off)
        for axis in range(2):
            for off in (0, 3, 1, 2):
                block = gathered.at[step, axis, 1, off]
                slot = (0, step, axis, 1, off)
                remote(block, block, gather_send.at[slot], gather_recv.at[slot], sibling).wait_recv()
                take(axis, 1, off)

        line_scalars = tree4([gathered[step, 0, 0, off, pl.ds(HALF, 8), :] for off in range(4)])
        line_scalars = line_scalars + tree4([gathered[step, 0, 1, off, pl.ds(HALF, 8), :] for off in range(4)])

        def wanted_sums(hits, axis, off, size):
            out = jnp.dot(hits[axis, pl.ds(off * size, size), :], rhs[axis], preferred_element_type=F32)
            out = out + pltpu.roll(out, TILE // 2, 1)
            return jnp.where(low_lanes[: size // 2], out[: size // 2], out[size // 2 :])

        for axis in range(2):
            for off in SIDES + (0,):
                sums_out[step, axis, off, pl.ds(0, HALF), :] = wanted_sums(slot_hits, axis, off, SLOTS)
                sums_out[step, axis, off, pl.ds(HALF, 8), :] = line_scalars
                if off:
                    slot = (step, axis, (-off) % 4)
                    copy = remote(
                        sums_out.at[step, axis, off],
                        sums_in.at[slot],
                        sums_send.at[slot],
                        sums_recv.at[slot],
                        line(1 - axis, off),
                    )
                    copy.start()
                    sent.append(copy)
        if first_step:
            mark_chunks()
        for axis in range(2):
            for off in SIDES + (0,):
                chunk_out[step, axis, off] = wanted_sums(chunk_hits, axis, off, CHUNK)
                if off:
                    slot = (step, axis, (-off) % 4)
                    copy = remote(
                        chunk_out.at[step, axis, off],
                        chunk_in.at[slot],
                        chunk_send.at[slot],
                        chunk_recv.at[slot],
                        line(1 - axis, off),
                    )
                    copy.start()
                    sent.append(copy)
        if not first_step:
            dense_three(0, dense_first, (0, 3, 1, 2))
        totals = []
        for axis in range(2):
            for off in (3, 1, 2):
                block = sums_in.at[step, axis, off]
                slot = (step, axis, off)
                remote(block, block, sums_send.at[slot], sums_recv.at[slot], sibling).wait_recv()
            totals.append(tree4([sums_out[step, axis, 0]] + [sums_in[step, axis, off] for off in (1, 2, 3)]))
        mine = jnp.concatenate(lane_swap(totals[0][:HALF], totals[1][:HALF]), axis=0)
        return mine, totals[0][HALF:]

    def chunk_sums(step):
        totals = []
        for axis in range(2):
            for off in (3, 1, 2):
                block = chunk_in.at[step, axis, off]
                slot = (step, axis, off)
                remote(block, block, chunk_send.at[slot], chunk_recv.at[slot], sibling).wait_recv()
            totals.append(tree4([chunk_out[step, axis, 0]] + [chunk_in[step, axis, off] for off in (1, 2, 3)]))
        return jnp.concatenate(lane_swap(totals[0], totals[1]), axis=0)

    def dense_one(step, dense, chunk):
        dense[at_x, at_z, core] = chunk
        for along in range(2):
            for side in SIDES:
                span = pl.ds(along * (CHUNK // 2), CHUNK // 2)
                block = dense.at[at_x, at_z, core, span]
                slot = (step, 0, along, (-side) % 4)
                device = peer(0, side) if along else peer(side, 0)
                copy = remote(block, block, dense_send.at[slot], dense_recv.at[slot], device)
                copy.start()
                sent.append(copy)

    def dense_two(step, dense):
        for along in range(2):
            span = pl.ds(along * (CHUNK // 2), CHUNK // 2)
            for off in (3, 1, 2):
                if along:
                    block = dense.at[at_x, (at_z + off) % 4, core, span]
                else:
                    block = dense.at[(at_x + off) % 4, at_z, core, span]
                remote(
                    block, block, dense_send.at[step, 0, along, off], dense_recv.at[step, 0, along, off], sibling
                ).wait_recv()
        for along in range(2):
            span = pl.ds(along * (CHUNK // 2), CHUNK // 2)
            for side in SIDES:
                block = dense.at[at_x, :, core, span] if along else dense.at[:, at_z, core, span]
                device = peer(side, 0) if along else peer(0, side)
                slot = (step, 1, along, (-side) % 4)
                copy = remote(block, block, dense_send.at[slot], dense_recv.at[slot], device)
                copy.start()
                sent.append(copy)

    def dense_three(step, dense, offs):
        for off in offs:
            for along in range(2):
                span = pl.ds(along * (CHUNK // 2), CHUNK // 2)
                if off == 0:
                    slot = (step, 2, along, 0)
                    block = dense.at[at_x, :, core, span] if along else dense.at[:, at_z, core, span]
                else:
                    slot = (step, 1, along, off)
                    if along:
                        block = dense.at[(at_x + off) % 4, :, core, span]
                    else:
                        block = dense.at[:, (at_z + off) % 4, core, span]
                    remote(block, block, dense_send.at[slot], dense_recv.at[slot], sibling).wait_recv()
                    slot = (step, 2, along, off)
                copy = remote(block, block, dense_send.at[slot], dense_recv.at[slot], sibling)
                copy.start()
                sent.append(copy)

    def dense_done(step, dense):
        for off in range(4):
            for along in range(2):
                span = pl.ds(along * (CHUNK // 2), CHUNK // 2)
                if along:
                    block = dense.at[(at_x + off) % 4, :, 1 - core, span]
                else:
                    block = dense.at[:, (at_z + off) % 4, 1 - core, span]
                slot = (step, 2, along, off)
                remote(block, block, dense_send.at[slot], dense_recv.at[slot], sibling).wait_recv()

    def image_start(step, image, scalars):
        image_out[step, pl.ds(0, ROW_BLOCKS), :] = image
        image_out[step, pl.ds(ROW_BLOCKS, 8), :] = scalar_rows(scalars)
        for side in SIDES:
            back = (-side) % 4
            copy = remote(
                image_out.at[step],
                image_in.at[step, back],
                image_send.at[step, back],
                image_recv.at[step, back],
                peer(0, 0, 0, side),
            )
            copy.start()
            sent.append(copy)

    def image_finish(step):
        for off in (3, 1, 2):
            block = image_in.at[step, off]
            remote(block, block, image_send.at[step, off], image_recv.at[step, off], sibling).wait_recv()
        parts = [image_out[step]] + [image_in[step, off] for off in (1, 2, 3)]
        total = tree4(parts)
        return total[:ROW_BLOCKS], total[ROW_BLOCKS:]

    def norm_sum(scalars, between):
        value = scalar_rows(scalars)
        norm_out[...] = value
        offs = [(x, z, c) for x in (2, 1, 3, 0) for z in (2, 1, 3, 0) for c in (1, 0) if (x, z, c) != (0, 0, 0)]
        for x, z, c in offs:
            slot = ((-x) % 4, (-z) % 4, c)
            copy = remote(norm_out, norm_in.at[slot], norm_send.at[slot], norm_recv.at[slot], peer(x, z, c))
            copy.start()
            sent.append(copy)
        between()
        for slot in offs:
            block = norm_in.at[slot]
            remote(block, block, norm_send.at[slot], norm_recv.at[slot], sibling).wait_recv()
        parts = {slot: norm_in[slot] for slot in offs}
        parts[0, 0, 0] = value
        lines = [
            tree4([tree4([parts[x, z, c] for x in range(4)]) for z in range(4)]) for c in range(2)
        ]
        return lines[0] + lines[1]

    def root(square):
        return jnp.sqrt(jnp.maximum(square, 0.0) + norm_eps)

    delays = delays_ref[...]
    pick_rows(delays)
    sums, scalars = back_and_gather(0, [total_of(delays * delays)], True)
    beta_first = root(scalars[0:1])
    right_first = sums / beta_first
    left_first = delays / beta_first

    def finish_first():
        chunk = chunk_sums(0) / beta_first
        dense_one(0, dense_first, chunk)
        return chunk

    image, chunk_first = forward(right_first, finish_first)
    image_start(0, image, [total_of(chunk_first * chunk_first)])
    dense_two(0, dense_first)
    image, scalars = image_finish(0)
    alpha_part = scalars[0:1, 0:1]

    pick_rows(image)
    scalars = [alpha_part, total_of(image * image), total_of(image * left_first), total_of(left_first * left_first)]
    sums, scalars = back_and_gather(1, scalars, False)
    alpha_first = root(scalars[0:1])
    beta_second = root(
        scalars[1:2] / (alpha_first * alpha_first) - 2.0 * scalars[2:3] + alpha_first * alpha_first * scalars[3:4]
    )
    left_second = (image / alpha_first - alpha_first * left_first) / beta_second

    def second_right(back, right):
        fresh = (back / alpha_first - alpha_first * right) / beta_second
        return fresh - beta_second * (right / alpha_first)

    def finish_second():
        chunk = second_right(chunk_sums(1), chunk_first)
        dense_one(1, dense_second, chunk)
        return chunk

    image, chunk_second = forward(second_right(sums, right_first), finish_second)
    image_start(1, image, [total_of(chunk_second * chunk_second)])
    dense_two(1, dense_second)
    image, scalars = image_finish(1)
    alpha_part = scalars[0:1, 0:1]
    scalars = [alpha_part, total_of(image * image), total_of(image * left_second), total_of(left_second * left_second)]
    scalars = norm_sum(scalars, lambda: dense_three(1, dense_second, (0, 3, 1, 2)))
    alpha_second = root(scalars[0:1])
    beta_third = root(
        scalars[1:2] / (alpha_second * alpha_second) - 2.0 * scalars[2:3] + alpha_second * alpha_second * scalars[3:4]
    )
    left_ref[...] = (image / alpha_second - alpha_second * left_second) / beta_third

    rho_first = jnp.sqrt(alpha_first * alpha_first + beta_second * beta_second)
    cosine = alpha_first / rho_first
    sine = beta_second / rho_first
    step_first = cosine * beta_first / rho_first
    phi_bar = sine * beta_first
    theta = sine * alpha_second
    rho_bar = -cosine * alpha_second
    rho_second = jnp.sqrt(rho_bar * rho_bar + beta_third * beta_third)
    step_second = rho_bar / rho_second * phi_bar / rho_second
    weight_first = (step_first - step_second * (theta / rho_first)) / alpha_first
    weight_second = step_second / alpha_second

    dense_done(0, dense_first)
    dense_done(1, dense_second)
    stores = []
    for off in range(4):
        for to_z in range(4):
            slow_buf[off, to_z] = dense_first[off, to_z] * weight_first + dense_second[off, to_z] * weight_second
        store = pltpu.make_async_copy(slow_buf.at[off], slow_hbm.at[off], store_sem.at[off])
        store.start()
        stores.append(store)
    for store in stores:
        store.wait()
    for copy in sent:
        copy.wait_send()


def shards(delays, kernel_tiles, row_blocks, col_blocks, tile_counts):
    dma = pltpu.SemaphoreType.DMA
    vmem = pl.BlockSpec(memory_space=pltpu.VMEM)
    hbm = pl.BlockSpec(memory_space=pltpu.HBM)
    anywhere = pl.BlockSpec(memory_space=pl.ANY)
    dense_shape = (4, 4, 2, CHUNK, TILE)
    slowness, left = pl.pallas_call(
        lsqr_kernel,
        out_shape=(
            jax.ShapeDtypeStruct(dense_shape, F32),
            jax.ShapeDtypeStruct((ROW_BLOCKS, TILE), F32),
        ),
        in_specs=[pl.BlockSpec(memory_space=pltpu.SMEM)] + [hbm] * 4,
        out_specs=(anywhere, vmem),
        scratch_shapes=[
            pltpu.VMEM((ROW_BLOCKS, TILE), F32),
            pltpu.VMEM((2, HALF), jnp.int32),
            pltpu.VMEM((2, HALF), jnp.int32),
            pltpu.VMEM((SLOTS * TILE, TILE), BF16),
            pltpu.VMEM((SLOTS, 2 * TILE), F32),
            pltpu.VMEM((SLOTS, TILE), F32),
            pltpu.VMEM((2, 2, 2, 4, BLOCK_ROWS, TILE), F32),
            pltpu.VMEM((2, 4 * SLOTS, TILE), F32),
            pltpu.VMEM((2, 4 * SLOTS, 8 * SLOTS), BF16),
            pltpu.VMEM((2, 4 * CHUNK, 8 * SLOTS), BF16),
            pltpu.VMEM((2, 8 * SLOTS, TILE), BF16),
            pltpu.VMEM((SLOTS, TILE), BF16),
            pltpu.VMEM((ROW_BLOCKS, SLOTS), BF16),
            pltpu.VMEM((2, 2, 4, 8, TILE), F32),
            pltpu.VMEM((2, 2, 4, BLOCK_ROWS, TILE), F32),
            pltpu.VMEM((2, 2, 4, BLOCK_ROWS, TILE), F32),
            pltpu.VMEM((2, 2, 4, CHUNK // 2, TILE), F32),
            pltpu.VMEM((2, 2, 4, CHUNK // 2, TILE), F32),
            pltpu.VMEM((2, ROW_BLOCKS + 8, TILE), F32),
            pltpu.VMEM((2, 4, ROW_BLOCKS + 8, TILE), F32),
            pltpu.VMEM((8, TILE), F32),
            pltpu.VMEM((4, 4, 2, 8, TILE), F32),
            pltpu.VMEM(dense_shape, F32),
            pltpu.VMEM(dense_shape, F32),
            pltpu.VMEM(dense_shape, F32),
            dma((LOAD_CHUNKS,)),
            dma((3,)),
            dma((4,)),
            dma((2, 2, 2, 2, 4)),
            dma((2, 2, 2, 2, 4)),
            dma((2, 2, 4)),
            dma((2, 2, 4)),
            dma((2, 2, 4)),
            dma((2, 2, 4)),
            dma((2, 2, 4)),
            dma((2, 2, 4)),
            dma((2, 4)),
            dma((2, 4)),
            dma((4, 4, 2)),
            dma((4, 4, 2)),
            dma((2, 3, 2, 4)),
            dma((2, 3, 2, 4)),
        ],
        compiler_params=pltpu.CompilerParams(
            collective_id=0, has_side_effects=True, vmem_limit_bytes=48 * 2**20
        ),
        cost_estimate=pl.CostEstimate(flops=2 * 10**9, bytes_accessed=12 * 2**20, transcendentals=0),
    )(
        tile_counts,
        delays.reshape(ROW_BLOCKS, TILE),
        row_blocks.reshape(2, HALF),
        col_blocks.reshape(2, HALF),
        kernel_tiles.reshape(SLOTS * TILE, TILE),
    )
    return slowness.reshape(-1), left.reshape(-1)


def solution(mesh):
    in_specs = (
        P("dp"),
        P("dp", "mp", None, None, None),
        P("dp", "mp", None),
        P("dp", "mp", None),
        P("dp", "mp"),
    )
    out_specs = (P("mp"), P("dp"))
    return jax.shard_map(shards, mesh=mesh, in_specs=in_specs, out_specs=out_specs, check_vma=False)
```

```python
import jax
import jax.numpy as jnp
from jax import lax
from jax.experimental import pallas as pl
from jax.experimental.pallas import tpu as pltpu
from jax.sharding import PartitionSpec as P

TILE = 128
SLOTS = 256
HALF = SLOTS // 2
ROW_BLOCKS = 64
CELL_BLOCKS = 4096
CHUNK = CELL_BLOCKS // 32
BLOCK_ROWS = HALF + 8
GROUP = 8
LOAD_CHUNKS = 8
norm_eps = 1e-06

MESH = pl.DeviceIdType.MESH
F32 = jnp.float32
BF16 = jnp.bfloat16
NT = (((1,), (1,)), ((), ()))

SIDES = (2, 1, 3)


def split_parts(values):
    high = values.astype(BF16)
    low = (values - high.astype(F32)).astype(BF16)
    return high, low


def side_by_side(values):
    return jnp.concatenate(split_parts(values), axis=1)


def total_of(values):
    return jnp.sum(jnp.sum(values, axis=0, keepdims=True), axis=1, keepdims=True)


def tree4(parts):
    return (parts[0] + parts[2]) + (parts[1] + parts[3])


def lsqr_kernel(
    count_ref,
    delays_hbm,
    rows_hbm,
    cols_hbm,
    tiles_hbm,
    dense_first,
    dense_second,
    weights_ref,
    left_ref,
    delays_ref,
    rows_ref,
    cols_ref,
    tiles,
    picked,
    slot_products,
    gathered,
    targets,
    slot_hits,
    chunk_hits,
    rhs,
    early,
    row_pick,
    row_sum,
    cols_line,
    sums_out,
    sums_in,
    chunk_out,
    chunk_in,
    image_out,
    image_in,
    norm_out,
    norm_in,
    chunk_buf,
    load_sem,
    small_sem,
    own_sem,
    gather_send,
    gather_recv,
    cols_send,
    cols_recv,
    sums_send,
    sums_recv,
    chunk_send,
    chunk_recv,
    image_send,
    image_recv,
    norm_send,
    norm_recv,
    dense_send,
    dense_recv,
):
    dp = lax.axis_index("dp")
    mp = lax.axis_index("mp")
    at_x, at_z, core = dp // 8, (dp // 2) % 4, dp % 2

    def peer(off_x, off_z, off_core=0, off_y=0):
        there = ((at_x + off_x) % 4) * 8 + ((at_z + off_z) % 4) * 2 + (core + off_core) % 2
        return (there, (mp + off_y) % 4)

    sibling = peer(0, 0, 1)

    def remote(src, dst, send, recv, device):
        return pltpu.make_async_remote_copy(
            src_ref=src, dst_ref=dst, send_sem=send, recv_sem=recv, device_id=device, device_id_type=MESH
        )

    smalls = []
    for number, (src, dst) in enumerate(((delays_hbm, delays_ref), (rows_hbm, rows_ref), (cols_hbm, cols_ref))):
        small = pltpu.make_async_copy(src, dst, small_sem.at[number])
        small.start()
        smalls.append(small)
    load_rows = SLOTS * TILE // LOAD_CHUNKS
    loads = [None] * LOAD_CHUNKS
    for part in [p for q in range(LOAD_CHUNKS // 2) for p in (q, q + LOAD_CHUNKS // 2)]:
        span = pl.ds(part * load_rows, load_rows)
        load = pltpu.make_async_copy(tiles_hbm.at[span], tiles.at[span], load_sem.at[part])
        load.start()
        loads[part] = load

    barrier = pltpu.get_barrier_semaphore()
    partners = [peer(side, 0) for side in SIDES] + [peer(0, side) for side in SIDES]
    partners += [sibling] + [peer(0, 0, 0, side) for side in SIDES]
    for partner in partners:
        pl.semaphore_signal(barrier, inc=1, device_id=partner, device_id_type=MESH)

    sent = []

    low_lanes = lax.broadcasted_iota(jnp.int32, (TILE, TILE), 1) < TILE // 2
    lane_f = lax.broadcasted_iota(jnp.int32, (TILE, TILE), 1).astype(F32)
    sub_i = lax.broadcasted_iota(jnp.int32, (TILE, TILE), 0)

    def lane_swap(first, second):
        low = low_lanes[: first.shape[0]]
        return (
            jnp.where(low, first, pltpu.roll(second, TILE // 2, 1)),
            jnp.where(low, pltpu.roll(first, TILE // 2, 1), second),
        )

    for small in smalls:
        small.wait()
    count = count_ref[0, 0]
    rows_f = rows_ref[...].astype(F32)
    cols_f = cols_ref[...].astype(F32)
    for half in range(2):
        down = jnp.transpose(jnp.broadcast_to(rows_f[half : half + 1, :], (TILE, TILE)))
        live = sub_i + half * HALF < count
        row_pick[pl.ds(half * HALF, HALF), :] = jnp.where((down == lane_f) & live, 1.0, 0.0).astype(BF16)
        across = jnp.broadcast_to(rows_f[half : half + 1, :], (ROW_BLOCKS, TILE))
        sub_r = lax.broadcasted_iota(jnp.int32, (ROW_BLOCKS, TILE), 0).astype(F32)
        lane_r = lax.broadcasted_iota(jnp.int32, (ROW_BLOCKS, TILE), 1) + half * HALF
        row_sum[:, pl.ds(half * HALF, HALF)] = jnp.where((across == sub_r) & (lane_r < count), 1.0, 0.0).astype(BF16)
    own_cols = jnp.concatenate([cols_f, jnp.zeros((6, TILE), F32)], axis=0)
    for axis in range(2):
        cols_line[axis, 0, 0] = own_cols

    def slot_targets(axis):
        wanted = jnp.concatenate([cols_line[1 - axis, 0, off, pl.ds(0, 2), :] for off in range(4)], axis=0)
        down = jnp.transpose(jnp.concatenate([wanted, jnp.zeros((TILE - 8, TILE), F32)], axis=0))
        for part in range(8):
            targets[axis, pl.ds(part * HALF, HALF), :] = jnp.broadcast_to(down[:, part : part + 1], (HALF, TILE))

    def pick_rows(vector):
        padded = jnp.concatenate([vector, jnp.zeros((TILE - ROW_BLOCKS, TILE), F32)], axis=0)
        picked[...] = jnp.dot(row_pick[...], side_by_side(padded), preferred_element_type=F32)

    row_in_group = lax.broadcasted_iota(jnp.int32, (2 * GROUP, TILE), 0) % GROUP
    sub_group = lax.broadcasted_iota(jnp.int32, (GROUP, TILE), 0)

    def both_parts(group):
        span = pl.ds(group * GROUP, GROUP)
        return jnp.concatenate([picked[span, pl.ds(0, TILE)], picked[span, pl.ds(TILE, TILE)]], axis=0)

    def back_group(group):
        parts = both_parts(group)
        lhs = jnp.concatenate(
            [jnp.where(row_in_group == slot, parts, 0.0).astype(BF16) for slot in range(GROUP)], axis=1
        )
        weights = tiles[pl.ds(group * (GROUP * TILE), GROUP * TILE), :]
        out = jnp.dot(lhs, weights, preferred_element_type=F32)
        return out[:GROUP] + out[GROUP:]

    def forward_group(group):
        lhs = both_parts(group).astype(BF16)
        weights = tiles[pl.ds(group * (GROUP * TILE), GROUP * TILE), :]
        out = lax.dot_general(lhs, weights, NT, preferred_element_type=F32)
        out = out[:GROUP] + out[GROUP:]
        chosen = out[:, :TILE]
        for slot in range(1, GROUP):
            chosen = jnp.where(sub_group == slot, out[:, slot * TILE : (slot + 1) * TILE], chosen)
        slot_products[pl.ds(group * GROUP, GROUP), :] = chosen

    def forward(right, between):
        high, low = split_parts(right)
        picked[:, pl.ds(0, TILE)] = high.astype(F32)
        picked[:, pl.ds(TILE, TILE)] = low.astype(F32)
        half = SLOTS // GROUP // 4

        @pl.loop(0, half, unroll=8)
        def _(group):
            forward_group(group)

        result = between()

        @pl.loop(half, 4 * half, unroll=8)
        def _(group):
            forward_group(group)

        out = jnp.dot(row_sum[...], side_by_side(slot_products[...]), preferred_element_type=F32)
        return out[:, :TILE] + out[:, TILE:], result

    def scalar_rows(scalars):
        rows = [jnp.broadcast_to(value, (1, TILE)) for value in scalars]
        rows += [jnp.zeros((8 - len(rows), TILE), F32)]
        return jnp.concatenate(rows, axis=0)

    def line(axis, off, core_off=0):
        return peer(0, off, core_off) if axis else peer(off, 0, core_off)

    def exchange_cols():
        copies = []
        for axis in range(2):
            for side in SIDES:
                back = (-side) % 4
                copy = remote(
                    cols_line.at[axis, 0, 0],
                    cols_line.at[axis, 0, back],
                    cols_send.at[axis, 0, back],
                    cols_recv.at[axis, 0, back],
                    line(axis, side),
                )
                copy.start()
                copies.append(copy)
        sent.extend(copies)
        return copies

    def mark(dst, axis, span, want, core_off):
        for off in range(4):
            for half in range(2):
                one = cols_line[axis, core_off, off, pl.ds(half, 1), :]
                column = ((core_off * 4 + off) * 2 + half) * HALF
                dst[axis, span, pl.ds(column, HALF)] = jnp.where(want == one, 1.0, 0.0).astype(BF16)

    def mark_slots(core_off):
        for axis in range(2):

            @pl.loop(0, 4 * SLOTS // TILE)
            def _(part):
                span = pl.ds(part * TILE, TILE)
                mark(slot_hits, axis, span, targets[axis, span, :], core_off)

    def mark_chunks():
        for axis in range(2):

            @pl.loop(0, 4)
            def _(off):
                device = peer(off, 0)[0] if axis else peer(0, off)[0]
                want = (sub_i + device * CHUNK).astype(F32)
                for core_off in range(2):
                    mark(chunk_hits, axis, pl.ds(off * CHUNK, CHUNK), want, core_off)

    def spread_cols(copies):
        for copy in copies:
            copy.wait_recv()
        across = []
        for axis in range(2):
            copy = remote(
                cols_line.at[axis, 0], cols_line.at[axis, 1], cols_send.at[axis, 1, 0], cols_recv.at[axis, 1, 0], sibling
            )
            copy.start()
            across.append(copy)
        sent.extend(across)
        for axis in range(2):
            slot_targets(axis)
        mark_slots(0)
        for copy in across:
            copy.wait_recv()
        mark_slots(1)

    def back_and_gather(step, scalars, first_step):
        def arrival(axis, off, piece):
            span = (pl.ds(0, HALF // 2), pl.ds(HALF // 2, BLOCK_ROWS - HALF // 2))[piece]
            block = gathered.at[step, axis, 0, off, span]
            slot = (piece, step, axis, 0, off)
            return remote(block, block, gather_send.at[slot], gather_recv.at[slot], sibling)

        tail = scalar_rows(scalars)
        for axis in range(2):
            gathered[step, axis, 0, 0, pl.ds(HALF, 8), :] = tail
        chunks = LOAD_CHUNKS // 2
        groups = HALF // GROUP
        per = groups // chunks
        def send(axis, to_off, device, piece):
            span = (pl.ds(0, HALF // 2), pl.ds(HALF // 2, BLOCK_ROWS - HALF // 2))[piece]
            copy = remote(
                gathered.at[step, axis, 0, 0, span],
                gathered.at[step, axis, 0, to_off, span],
                gather_send.at[piece, step, axis, 0, to_off],
                gather_recv.at[piece, step, axis, 0, to_off],
                device,
            )
            copy.start()
            sent.append(copy)

        def across(axis, off):
            block = gathered.at[step, axis, 0, off]
            slot = (0, step, axis, 1, off)
            copy = remote(block, gathered.at[step, axis, 1, off], gather_send.at[slot], gather_recv.at[slot], sibling)
            copy.start()
            sent.append(copy)

        for part in range(chunks):
            if first_step:
                loads[part].wait()
                loads[chunks + part].wait()

            @pl.loop(0, per, unroll=per)
            def _(index):
                group = part * per + index
                low, high = lane_swap(back_group(group), back_group(groups + group))
                span = pl.ds(group * GROUP, GROUP)
                gathered[step, 0, 0, 0, span, :] = low
                gathered[step, 1, 0, 0, span, :] = high

            if 2 * (part + 1) % chunks == 0:
                piece = 2 * (part + 1) // chunks - 1
                if first_step and piece == 0:
                    pl.semaphore_wait(barrier, len(partners))
                    cols_copies = exchange_cols()
                for side in SIDES:
                    for axis in range(2):
                        send(axis, (-side) % 4, line(axis, side), piece)
        for axis in range(2):
            across(axis, 0)
        if first_step:
            spread_cols(cols_copies)
        for off in (3, 1, 2):
            for axis in range(2):
                for piece in range(2):
                    arrival(axis, off, piece).wait_recv()
                across(axis, off)

        def take(axis, core_off, off):
            block = gathered[step, axis, core_off, off, pl.ds(0, HALF), :]
            high = block.astype(BF16).astype(F32)
            first, second = lane_swap(high, block - high)
            row = (core_off * 4 + off) * SLOTS
            rhs[axis, pl.ds(row, HALF), :] = first.astype(BF16)
            rhs[axis, pl.ds(row + HALF, HALF), :] = second.astype(BF16)

        def half_dot(hits, axis, off, size, part):
            span = pl.ds(part * (4 * SLOTS), 4 * SLOTS)
            return jnp.dot(hits[axis, pl.ds(off * size, size), span], rhs[axis, span, :], preferred_element_type=F32)

        def packed(out):
            size = out.shape[0]
            out = out + pltpu.roll(out, TILE // 2, 1)
            return jnp.where(low_lanes[: size // 2], out[: size // 2], out[size // 2 :])

        def slot_sums(axis, off):
            return packed(early[axis, off] + half_dot(slot_hits, axis, off, SLOTS, 1))

        def chunk_part(axis, off):
            span = pl.ds(off * CHUNK, CHUNK)
            return packed(jnp.dot(chunk_hits[axis, span, :], rhs[axis], preferred_element_type=F32))

        for axis in range(2):
            for off in range(4):
                take(axis, 0, off)
        for axis in range(2):
            for off in SIDES + (0,):
                early[axis, off] = half_dot(slot_hits, axis, off, SLOTS, 0)
        for axis in range(2):
            for off in (0, 3, 1, 2):
                block = gathered.at[step, axis, 1, off]
                slot = (0, step, axis, 1, off)
                remote(block, block, gather_send.at[slot], gather_recv.at[slot], sibling).wait_recv()
                take(axis, 1, off)

        line_scalars = tree4([gathered[step, 0, 0, off, pl.ds(HALF, 8), :] for off in range(4)])
        line_scalars = line_scalars + tree4([gathered[step, 0, 1, off, pl.ds(HALF, 8), :] for off in range(4)])

        for axis in range(2):
            for off in SIDES:
                sums_out[step, axis, off, pl.ds(0, HALF), :] = slot_sums(axis, off)
                sums_out[step, axis, off, pl.ds(HALF, 8), :] = line_scalars
                slot = (step, axis, (-off) % 4)
                copy = remote(
                    sums_out.at[step, axis, off],
                    sums_in.at[slot],
                    sums_send.at[slot],
                    sums_recv.at[slot],
                    line(1 - axis, off),
                )
                copy.start()
                sent.append(copy)
        if first_step:
            mark_chunks()
        for axis in range(2):
            for off in SIDES:
                chunk_out[step, axis, off] = chunk_part(axis, off)
                slot = (step, axis, (-off) % 4)
                copy = remote(
                    chunk_out.at[step, axis, off],
                    chunk_in.at[slot],
                    chunk_send.at[slot],
                    chunk_recv.at[slot],
                    line(1 - axis, off),
                )
                copy.start()
                sent.append(copy)
        for axis in range(2):
            sums_out[step, axis, 0, pl.ds(0, HALF), :] = slot_sums(axis, 0)
            sums_out[step, axis, 0, pl.ds(HALF, 8), :] = line_scalars
            chunk_out[step, axis, 0] = chunk_part(axis, 0)
        if not first_step:
            dense_three(0, dense_first, (0, 3, 1, 2))
        totals = []
        for axis in range(2):
            for off in (3, 1, 2):
                block = sums_in.at[step, axis, off]
                slot = (step, axis, off)
                remote(block, block, sums_send.at[slot], sums_recv.at[slot], sibling).wait_recv()
            totals.append(tree4([sums_out[step, axis, 0]] + [sums_in[step, axis, off] for off in (1, 2, 3)]))
        mine = jnp.concatenate(lane_swap(totals[0][:HALF], totals[1][:HALF]), axis=0)
        return mine, totals[0][HALF:]

    def chunk_sums(step):
        totals = []
        for axis in range(2):
            for off in (3, 1, 2):
                block = chunk_in.at[step, axis, off]
                slot = (step, axis, off)
                remote(block, block, chunk_send.at[slot], chunk_recv.at[slot], sibling).wait_recv()
            totals.append(tree4([chunk_out[step, axis, 0]] + [chunk_in[step, axis, off] for off in (1, 2, 3)]))
        return jnp.concatenate(lane_swap(totals[0], totals[1]), axis=0)

    def dense_one(step, dense, chunk):
        chunk_buf[step] = chunk
        own = pltpu.make_async_copy(chunk_buf.at[step], dense.at[at_x, at_z, core], own_sem.at[step])
        own.start()
        for along in range(2):
            for side in SIDES:
                span = pl.ds(along * (CHUNK // 2), CHUNK // 2)
                block = dense.at[at_x, at_z, core, span]
                slot = (step, 0, along, (-side) % 4)
                device = peer(0, side) if along else peer(side, 0)
                copy = remote(chunk_buf.at[step, span], block, dense_send.at[slot], dense_recv.at[slot], device)
                copy.start()
                sent.append(copy)
        own.wait()

    def dense_two(step, dense):
        for along in range(2):
            span = pl.ds(along * (CHUNK // 2), CHUNK // 2)
            for off in (3, 1, 2):
                if along:
                    block = dense.at[at_x, (at_z + off) % 4, core, span]
                else:
                    block = dense.at[(at_x + off) % 4, at_z, core, span]
                remote(
                    block, block, dense_send.at[step, 0, along, off], dense_recv.at[step, 0, along, off], sibling
                ).wait_recv()
        for along in range(2):
            span = pl.ds(along * (CHUNK // 2), CHUNK // 2)
            for side in SIDES:
                block = dense.at[at_x, :, core, span] if along else dense.at[:, at_z, core, span]
                device = peer(side, 0) if along else peer(0, side)
                slot = (step, 1, along, (-side) % 4)
                copy = remote(block, block, dense_send.at[slot], dense_recv.at[slot], device)
                copy.start()
                sent.append(copy)

    def dense_three(step, dense, offs):
        for off in offs:
            for along in range(2):
                span = pl.ds(along * (CHUNK // 2), CHUNK // 2)
                if off == 0:
                    slot = (step, 2, along, 0)
                    block = dense.at[at_x, :, core, span] if along else dense.at[:, at_z, core, span]
                else:
                    slot = (step, 1, along, off)
                    if along:
                        block = dense.at[(at_x + off) % 4, :, core, span]
                    else:
                        block = dense.at[:, (at_z + off) % 4, core, span]
                    remote(block, block, dense_send.at[slot], dense_recv.at[slot], sibling).wait_recv()
                    slot = (step, 2, along, off)
                copy = remote(block, block, dense_send.at[slot], dense_recv.at[slot], sibling)
                copy.start()
                sent.append(copy)

    def dense_done(step, dense):
        for off in range(4):
            for along in range(2):
                span = pl.ds(along * (CHUNK // 2), CHUNK // 2)
                if along:
                    block = dense.at[(at_x + off) % 4, :, 1 - core, span]
                else:
                    block = dense.at[:, (at_z + off) % 4, 1 - core, span]
                slot = (step, 2, along, off)
                remote(block, block, dense_send.at[slot], dense_recv.at[slot], sibling).wait_recv()

    def image_start(step, image, scalars):
        image_out[step, pl.ds(0, ROW_BLOCKS), :] = image
        image_out[step, pl.ds(ROW_BLOCKS, 8), :] = scalar_rows(scalars)
        for side in SIDES:
            back = (-side) % 4
            copy = remote(
                image_out.at[step],
                image_in.at[step, back],
                image_send.at[step, back],
                image_recv.at[step, back],
                peer(0, 0, 0, side),
            )
            copy.start()
            sent.append(copy)

    def image_finish(step):
        for off in (3, 1, 2):
            block = image_in.at[step, off]
            remote(block, block, image_send.at[step, off], image_recv.at[step, off], sibling).wait_recv()
        parts = [image_out[step]] + [image_in[step, off] for off in (1, 2, 3)]
        total = tree4(parts)
        return total[:ROW_BLOCKS], total[ROW_BLOCKS:]

    def norm_sum(scalars, between):
        value = scalar_rows(scalars)
        norm_out[...] = value
        offs = [(x, z, c) for x in (2, 1, 3, 0) for z in (2, 1, 3, 0) for c in (1, 0) if (x, z, c) != (0, 0, 0)]
        for x, z, c in offs:
            slot = ((-x) % 4, (-z) % 4, c)
            copy = remote(norm_out, norm_in.at[slot], norm_send.at[slot], norm_recv.at[slot], peer(x, z, c))
            copy.start()
            sent.append(copy)
        between()
        for slot in offs:
            block = norm_in.at[slot]
            remote(block, block, norm_send.at[slot], norm_recv.at[slot], sibling).wait_recv()
        parts = {slot: norm_in[slot] for slot in offs}
        parts[0, 0, 0] = value
        lines = [
            tree4([tree4([parts[x, z, c] for x in range(4)]) for z in range(4)]) for c in range(2)
        ]
        return lines[0] + lines[1]

    def root(square):
        return jnp.sqrt(jnp.maximum(square, 0.0) + norm_eps)

    delays = delays_ref[...]
    pick_rows(delays)
    sums, scalars = back_and_gather(0, [total_of(delays * delays)], True)
    beta_first = root(scalars[0:1])
    right_first = sums / beta_first
    left_first = delays / beta_first

    def finish_first():
        chunk = chunk_sums(0) / beta_first
        dense_one(0, dense_first, chunk)
        return chunk

    image, chunk_first = forward(right_first, finish_first)
    image_start(0, image, [total_of(chunk_first * chunk_first)])
    dense_two(0, dense_first)
    image, scalars = image_finish(0)
    alpha_part = scalars[0:1, 0:1]

    pick_rows(image)
    scalars = [alpha_part, total_of(image * image), total_of(image * left_first), total_of(left_first * left_first)]
    sums, scalars = back_and_gather(1, scalars, False)
    alpha_first = root(scalars[0:1])
    beta_second = root(
        scalars[1:2] / (alpha_first * alpha_first) - 2.0 * scalars[2:3] + alpha_first * alpha_first * scalars[3:4]
    )
    left_second = (image / alpha_first - alpha_first * left_first) / beta_second

    def second_right(back, right):
        fresh = (back / alpha_first - alpha_first * right) / beta_second
        return fresh - beta_second * (right / alpha_first)

    def finish_second():
        chunk = second_right(chunk_sums(1), chunk_first)
        dense_one(1, dense_second, chunk)
        return chunk

    image, chunk_second = forward(second_right(sums, right_first), finish_second)
    image_start(1, image, [total_of(chunk_second * chunk_second)])
    dense_two(1, dense_second)
    image, scalars = image_finish(1)
    alpha_part = scalars[0:1, 0:1]
    scalars = [alpha_part, total_of(image * image), total_of(image * left_second), total_of(left_second * left_second)]
    scalars = norm_sum(scalars, lambda: dense_three(1, dense_second, (0, 3, 1, 2)))
    alpha_second = root(scalars[0:1])
    beta_third = root(
        scalars[1:2] / (alpha_second * alpha_second) - 2.0 * scalars[2:3] + alpha_second * alpha_second * scalars[3:4]
    )
    left_ref[...] = (image / alpha_second - alpha_second * left_second) / beta_third

    rho_first = jnp.sqrt(alpha_first * alpha_first + beta_second * beta_second)
    cosine = alpha_first / rho_first
    sine = beta_second / rho_first
    step_first = cosine * beta_first / rho_first
    phi_bar = sine * beta_first
    theta = sine * alpha_second
    rho_bar = -cosine * alpha_second
    rho_second = jnp.sqrt(rho_bar * rho_bar + beta_third * beta_third)
    step_second = rho_bar / rho_second * phi_bar / rho_second
    weight_first = (step_first - step_second * (theta / rho_first)) / alpha_first
    weight_second = step_second / alpha_second

    dense_done(0, dense_first)
    dense_done(1, dense_second)
    weights_ref[...] = scalar_rows([weight_first, weight_second])
    for copy in sent:
        copy.wait_send()


def combine_kernel(first, second, weights, left, slow_hbm, left_hbm, buffer, sems):
    copies = [pltpu.make_async_copy(left, left_hbm, sems.at[4])]
    copies[0].start()
    weight_first, weight_second = weights[0:1, :], weights[1:2, :]
    for off in range(4):
        for to_z in range(4):
            buffer[off, to_z] = first[off, to_z] * weight_first + second[off, to_z] * weight_second
        copy = pltpu.make_async_copy(buffer.at[off], slow_hbm.at[off], sems.at[off])
        copy.start()
        copies.append(copy)
    for copy in copies:
        copy.wait()


def shards(delays, kernel_tiles, row_blocks, col_blocks, tile_counts):
    dma = pltpu.SemaphoreType.DMA
    vmem = pl.BlockSpec(memory_space=pltpu.VMEM)
    hbm = pl.BlockSpec(memory_space=pltpu.HBM)
    anywhere = pl.BlockSpec(memory_space=pl.ANY)
    dense_shape = (4, 4, 2, CHUNK, TILE)
    first, second, weights, left = pl.pallas_call(
        lsqr_kernel,
        out_shape=(
            jax.ShapeDtypeStruct(dense_shape, F32),
            jax.ShapeDtypeStruct(dense_shape, F32),
            jax.ShapeDtypeStruct((8, TILE), F32),
            jax.ShapeDtypeStruct((ROW_BLOCKS, TILE), F32),
        ),
        in_specs=[pl.BlockSpec(memory_space=pltpu.SMEM)] + [hbm] * 4,
        out_specs=(anywhere, anywhere, vmem, vmem),
        scratch_shapes=[
            pltpu.VMEM((ROW_BLOCKS, TILE), F32),
            pltpu.VMEM((2, HALF), jnp.int32),
            pltpu.VMEM((2, HALF), jnp.int32),
            pltpu.VMEM((SLOTS * TILE, TILE), BF16),
            pltpu.VMEM((SLOTS, 2 * TILE), F32),
            pltpu.VMEM((SLOTS, TILE), F32),
            pltpu.VMEM((2, 2, 2, 4, BLOCK_ROWS, TILE), F32),
            pltpu.VMEM((2, 4 * SLOTS, TILE), F32),
            pltpu.VMEM((2, 4 * SLOTS, 8 * SLOTS), BF16),
            pltpu.VMEM((2, 4 * CHUNK, 8 * SLOTS), BF16),
            pltpu.VMEM((2, 8 * SLOTS, TILE), BF16),
            pltpu.VMEM((2, 4, SLOTS, TILE), F32),
            pltpu.VMEM((SLOTS, TILE), BF16),
            pltpu.VMEM((ROW_BLOCKS, SLOTS), BF16),
            pltpu.VMEM((2, 2, 4, 8, TILE), F32),
            pltpu.VMEM((2, 2, 4, BLOCK_ROWS, TILE), F32),
            pltpu.VMEM((2, 2, 4, BLOCK_ROWS, TILE), F32),
            pltpu.VMEM((2, 2, 4, CHUNK // 2, TILE), F32),
            pltpu.VMEM((2, 2, 4, CHUNK // 2, TILE), F32),
            pltpu.VMEM((2, ROW_BLOCKS + 8, TILE), F32),
            pltpu.VMEM((2, 4, ROW_BLOCKS + 8, TILE), F32),
            pltpu.VMEM((8, TILE), F32),
            pltpu.VMEM((4, 4, 2, 8, TILE), F32),
            pltpu.VMEM((2, CHUNK, TILE), F32),
            dma((LOAD_CHUNKS,)),
            dma((3,)),
            dma((2,)),
            dma((2, 2, 2, 2, 4)),
            dma((2, 2, 2, 2, 4)),
            dma((2, 2, 4)),
            dma((2, 2, 4)),
            dma((2, 2, 4)),
            dma((2, 2, 4)),
            dma((2, 2, 4)),
            dma((2, 2, 4)),
            dma((2, 4)),
            dma((2, 4)),
            dma((4, 4, 2)),
            dma((4, 4, 2)),
            dma((2, 3, 2, 4)),
            dma((2, 3, 2, 4)),
        ],
        compiler_params=pltpu.CompilerParams(
            collective_id=0, has_side_effects=True, vmem_limit_bytes=48 * 2**20
        ),
        cost_estimate=pl.CostEstimate(flops=2 * 10**9, bytes_accessed=12 * 2**20, transcendentals=0),
    )(
        tile_counts,
        delays.reshape(ROW_BLOCKS, TILE),
        row_blocks.reshape(2, HALF),
        col_blocks.reshape(2, HALF),
        kernel_tiles.reshape(SLOTS * TILE, TILE),
    )
    slowness, left = pl.pallas_call(
        combine_kernel,
        out_shape=(
            jax.ShapeDtypeStruct(dense_shape, F32),
            jax.ShapeDtypeStruct((ROW_BLOCKS, TILE), F32),
        ),
        in_specs=[vmem] * 4,
        out_specs=(anywhere, anywhere),
        scratch_shapes=[pltpu.VMEM(dense_shape, F32), dma((5,))],
        compiler_params=pltpu.CompilerParams(vmem_limit_bytes=8 * 2**20),
        cost_estimate=pl.CostEstimate(flops=2**20, bytes_accessed=6 * 2**20, transcendentals=0),
    )(first, second, weights, left)
    return slowness.reshape(-1), left.reshape(-1)


def solution(mesh):
    in_specs = (
        P("dp"),
        P("dp", "mp", None, None, None),
        P("dp", "mp", None),
        P("dp", "mp", None),
        P("dp", "mp"),
    )
    out_specs = (P("mp"), P("dp"))
    return jax.shard_map(shards, mesh=mesh, in_specs=in_specs, out_specs=out_specs, check_vma=False)
```

```python
import jax
import jax.numpy as jnp
from jax import lax
from jax.experimental import pallas as pl
from jax.experimental.pallas import tpu as pltpu
from jax.sharding import PartitionSpec as P

TILE = 128
SLOTS = 256
HALF = SLOTS // 2
ROW_BLOCKS = 64
CELL_BLOCKS = 4096
CHUNK = CELL_BLOCKS // 32
BLOCK_ROWS = HALF + 8
GROUP = 8
LOAD_CHUNKS = 8
norm_eps = 1e-06

MESH = pl.DeviceIdType.MESH
F32 = jnp.float32
BF16 = jnp.bfloat16
NT = (((1,), (1,)), ((), ()))

SIDES = (2, 1, 3)


def split_parts(values):
    high = values.astype(BF16)
    low = (values - high.astype(F32)).astype(BF16)
    return high, low


def side_by_side(values):
    return jnp.concatenate(split_parts(values), axis=1)


def total_of(values):
    return jnp.sum(jnp.sum(values, axis=0, keepdims=True), axis=1, keepdims=True)


def tree4(parts):
    return (parts[0] + parts[2]) + (parts[1] + parts[3])


def lsqr_kernel(
    count_ref,
    delays_hbm,
    rows_hbm,
    cols_hbm,
    tiles_hbm,
    dense_first,
    dense_second,
    weights_ref,
    left_ref,
    delays_ref,
    rows_ref,
    cols_ref,
    tiles,
    picked,
    slot_products,
    gathered,
    targets,
    slot_hits,
    chunk_hits,
    rhs,
    early,
    early_chunk,
    row_pick,
    row_sum,
    cols_line,
    sums_out,
    sums_in,
    chunk_out,
    chunk_in,
    image_out,
    image_in,
    norm_out,
    norm_in,
    chunk_buf,
    load_sem,
    small_sem,
    own_sem,
    gather_send,
    gather_recv,
    cols_send,
    cols_recv,
    sums_send,
    sums_recv,
    chunk_send,
    chunk_recv,
    image_send,
    image_recv,
    norm_send,
    norm_recv,
    dense_send,
    dense_recv,
):
    dp = lax.axis_index("dp")
    mp = lax.axis_index("mp")
    at_x, at_z, core = dp // 8, (dp // 2) % 4, dp % 2

    def peer(off_x, off_z, off_core=0, off_y=0):
        there = ((at_x + off_x) % 4) * 8 + ((at_z + off_z) % 4) * 2 + (core + off_core) % 2
        return (there, (mp + off_y) % 4)

    sibling = peer(0, 0, 1)

    def remote(src, dst, send, recv, device):
        return pltpu.make_async_remote_copy(
            src_ref=src, dst_ref=dst, send_sem=send, recv_sem=recv, device_id=device, device_id_type=MESH
        )

    smalls = []
    for number, (src, dst) in enumerate(((delays_hbm, delays_ref), (rows_hbm, rows_ref), (cols_hbm, cols_ref))):
        small = pltpu.make_async_copy(src, dst, small_sem.at[number])
        small.start()
        smalls.append(small)
    load_rows = SLOTS * TILE // LOAD_CHUNKS
    loads = [None] * LOAD_CHUNKS
    for part in [p for q in range(LOAD_CHUNKS // 2) for p in (q, q + LOAD_CHUNKS // 2)]:
        span = pl.ds(part * load_rows, load_rows)
        load = pltpu.make_async_copy(tiles_hbm.at[span], tiles.at[span], load_sem.at[part])
        load.start()
        loads[part] = load

    barrier = pltpu.get_barrier_semaphore()
    partners = [peer(side, 0) for side in SIDES] + [peer(0, side) for side in SIDES]
    partners += [sibling] + [peer(0, 0, 0, side) for side in SIDES]
    for partner in partners:
        pl.semaphore_signal(barrier, inc=1, device_id=partner, device_id_type=MESH)

    sent = []

    low_lanes = lax.broadcasted_iota(jnp.int32, (TILE, TILE), 1) < TILE // 2
    lane_f = lax.broadcasted_iota(jnp.int32, (TILE, TILE), 1).astype(F32)
    sub_i = lax.broadcasted_iota(jnp.int32, (TILE, TILE), 0)

    def lane_swap(first, second):
        low = low_lanes[: first.shape[0]]
        return (
            jnp.where(low, first, pltpu.roll(second, TILE // 2, 1)),
            jnp.where(low, pltpu.roll(first, TILE // 2, 1), second),
        )

    for small in smalls:
        small.wait()
    count = count_ref[0, 0]
    rows_f = rows_ref[...].astype(F32)
    cols_f = cols_ref[...].astype(F32)
    for half in range(2):
        down = jnp.transpose(jnp.broadcast_to(rows_f[half : half + 1, :], (TILE, TILE)))
        live = sub_i + half * HALF < count
        row_pick[pl.ds(half * HALF, HALF), :] = jnp.where((down == lane_f) & live, 1.0, 0.0).astype(BF16)
        across = jnp.broadcast_to(rows_f[half : half + 1, :], (ROW_BLOCKS, TILE))
        sub_r = lax.broadcasted_iota(jnp.int32, (ROW_BLOCKS, TILE), 0).astype(F32)
        lane_r = lax.broadcasted_iota(jnp.int32, (ROW_BLOCKS, TILE), 1) + half * HALF
        row_sum[:, pl.ds(half * HALF, HALF)] = jnp.where((across == sub_r) & (lane_r < count), 1.0, 0.0).astype(BF16)
    own_cols = jnp.concatenate([cols_f, jnp.zeros((6, TILE), F32)], axis=0)
    for axis in range(2):
        cols_line[axis, 0, 0] = own_cols

    def slot_targets(axis):
        wanted = jnp.concatenate([cols_line[1 - axis, 0, off, pl.ds(0, 2), :] for off in range(4)], axis=0)
        down = jnp.transpose(jnp.concatenate([wanted, jnp.zeros((TILE - 8, TILE), F32)], axis=0))
        for part in range(8):
            targets[axis, pl.ds(part * HALF, HALF), :] = jnp.broadcast_to(down[:, part : part + 1], (HALF, TILE))

    def pick_rows(vector):
        padded = jnp.concatenate([vector, jnp.zeros((TILE - ROW_BLOCKS, TILE), F32)], axis=0)
        picked[...] = jnp.dot(row_pick[...], side_by_side(padded), preferred_element_type=F32)

    row_in_group = lax.broadcasted_iota(jnp.int32, (2 * GROUP, TILE), 0) % GROUP
    sub_group = lax.broadcasted_iota(jnp.int32, (GROUP, TILE), 0)

    def both_parts(group):
        span = pl.ds(group * GROUP, GROUP)
        return jnp.concatenate([picked[span, pl.ds(0, TILE)], picked[span, pl.ds(TILE, TILE)]], axis=0)

    def back_group(group):
        parts = both_parts(group)
        lhs = jnp.concatenate(
            [jnp.where(row_in_group == slot, parts, 0.0).astype(BF16) for slot in range(GROUP)], axis=1
        )
        weights = tiles[pl.ds(group * (GROUP * TILE), GROUP * TILE), :]
        out = jnp.dot(lhs, weights, preferred_element_type=F32)
        return out[:GROUP] + out[GROUP:]

    def forward_group(group):
        lhs = both_parts(group).astype(BF16)
        weights = tiles[pl.ds(group * (GROUP * TILE), GROUP * TILE), :]
        out = lax.dot_general(lhs, weights, NT, preferred_element_type=F32)
        out = out[:GROUP] + out[GROUP:]
        chosen = out[:, :TILE]
        for slot in range(1, GROUP):
            chosen = jnp.where(sub_group == slot, out[:, slot * TILE : (slot + 1) * TILE], chosen)
        slot_products[pl.ds(group * GROUP, GROUP), :] = chosen

    def forward(right, between):
        high, low = split_parts(right)
        picked[:, pl.ds(0, TILE)] = high.astype(F32)
        picked[:, pl.ds(TILE, TILE)] = low.astype(F32)
        half = SLOTS // GROUP // 4

        @pl.loop(0, half, unroll=8)
        def _(group):
            forward_group(group)

        result = between()

        @pl.loop(half, 4 * half, unroll=8)
        def _(group):
            forward_group(group)

        out = jnp.dot(row_sum[...], side_by_side(slot_products[...]), preferred_element_type=F32)
        return out[:, :TILE] + out[:, TILE:], result

    def scalar_rows(scalars):
        rows = [jnp.broadcast_to(value, (1, TILE)) for value in scalars]
        rows += [jnp.zeros((8 - len(rows), TILE), F32)]
        return jnp.concatenate(rows, axis=0)

    def line(axis, off, core_off=0):
        return peer(0, off, core_off) if axis else peer(off, 0, core_off)

    def exchange_cols():
        copies = []
        for axis in range(2):
            for side in SIDES:
                back = (-side) % 4
                copy = remote(
                    cols_line.at[axis, 0, 0],
                    cols_line.at[axis, 0, back],
                    cols_send.at[axis, 0, back],
                    cols_recv.at[axis, 0, back],
                    line(axis, side),
                )
                copy.start()
                copies.append(copy)
        sent.extend(copies)
        return copies

    def mark(dst, axis, span, want, core_off):
        for off in range(4):
            for half in range(2):
                one = cols_line[axis, core_off, off, pl.ds(half, 1), :]
                column = ((core_off * 4 + off) * 2 + half) * HALF
                dst[axis, span, pl.ds(column, HALF)] = jnp.where(want == one, 1.0, 0.0).astype(BF16)

    def mark_slots(core_off):
        for axis in range(2):

            @pl.loop(0, 4 * SLOTS // TILE)
            def _(part):
                span = pl.ds(part * TILE, TILE)
                mark(slot_hits, axis, span, targets[axis, span, :], core_off)

    def mark_chunks():
        for axis in range(2):

            @pl.loop(0, 4)
            def _(off):
                device = peer(off, 0)[0] if axis else peer(0, off)[0]
                want = (sub_i + device * CHUNK).astype(F32)
                for core_off in range(2):
                    mark(chunk_hits, axis, pl.ds(off * CHUNK, CHUNK), want, core_off)

    def spread_cols(copies):
        for copy in copies:
            copy.wait_recv()
        across = []
        for axis in range(2):
            copy = remote(
                cols_line.at[axis, 0], cols_line.at[axis, 1], cols_send.at[axis, 1, 0], cols_recv.at[axis, 1, 0], sibling
            )
            copy.start()
            across.append(copy)
        sent.extend(across)
        for axis in range(2):
            slot_targets(axis)
        mark_slots(0)
        for copy in across:
            copy.wait_recv()
        mark_slots(1)

    def back_and_gather(step, scalars, first_step):
        def arrival(axis, off, piece):
            span = (pl.ds(0, HALF // 2), pl.ds(HALF // 2, BLOCK_ROWS - HALF // 2))[piece]
            block = gathered.at[step, axis, 0, off, span]
            slot = (piece, step, axis, 0, off)
            return remote(block, block, gather_send.at[slot], gather_recv.at[slot], sibling)

        tail = scalar_rows(scalars)
        for axis in range(2):
            gathered[step, axis, 0, 0, pl.ds(HALF, 8), :] = tail
        chunks = LOAD_CHUNKS // 2
        groups = HALF // GROUP
        per = groups // chunks
        def send(axis, to_off, device, piece):
            span = (pl.ds(0, HALF // 2), pl.ds(HALF // 2, BLOCK_ROWS - HALF // 2))[piece]
            copy = remote(
                gathered.at[step, axis, 0, 0, span],
                gathered.at[step, axis, 0, to_off, span],
                gather_send.at[piece, step, axis, 0, to_off],
                gather_recv.at[piece, step, axis, 0, to_off],
                device,
            )
            copy.start()
            sent.append(copy)

        def across(axis, off):
            block = gathered.at[step, axis, 0, off]
            slot = (0, step, axis, 1, off)
            copy = remote(block, gathered.at[step, axis, 1, off], gather_send.at[slot], gather_recv.at[slot], sibling)
            copy.start()
            sent.append(copy)

        for part in range(chunks):
            if first_step:
                loads[part].wait()
                loads[chunks + part].wait()

            @pl.loop(0, per, unroll=per)
            def _(index):
                group = part * per + index
                low, high = lane_swap(back_group(group), back_group(groups + group))
                span = pl.ds(group * GROUP, GROUP)
                gathered[step, 0, 0, 0, span, :] = low
                gathered[step, 1, 0, 0, span, :] = high

            if 2 * (part + 1) % chunks == 0:
                piece = 2 * (part + 1) // chunks - 1
                if first_step and piece == 0:
                    pl.semaphore_wait(barrier, len(partners))
                    cols_copies = exchange_cols()
                for side in SIDES:
                    for axis in range(2):
                        send(axis, (-side) % 4, line(axis, side), piece)
        for axis in range(2):
            across(axis, 0)
        if first_step:
            spread_cols(cols_copies)
        for off in (3, 1, 2):
            for axis in range(2):
                for piece in range(2):
                    arrival(axis, off, piece).wait_recv()
                across(axis, off)

        def take(axis, core_off, off):
            block = gathered[step, axis, core_off, off, pl.ds(0, HALF), :]
            high = block.astype(BF16).astype(F32)
            first, second = lane_swap(high, block - high)
            row = (core_off * 4 + off) * SLOTS
            rhs[axis, pl.ds(row, HALF), :] = first.astype(BF16)
            rhs[axis, pl.ds(row + HALF, HALF), :] = second.astype(BF16)

        def half_dot(hits, axis, off, size, part):
            span = pl.ds(part * (4 * SLOTS), 4 * SLOTS)
            return jnp.dot(hits[axis, pl.ds(off * size, size), span], rhs[axis, span, :], preferred_element_type=F32)

        def packed(out):
            size = out.shape[0]
            out = out + pltpu.roll(out, TILE // 2, 1)
            return jnp.where(low_lanes[: size // 2], out[: size // 2], out[size // 2 :])

        def slot_sums(axis, off):
            return packed(early[axis, off] + half_dot(slot_hits, axis, off, SLOTS, 1))

        def chunk_part(axis, off):
            if first_step:
                return packed(half_dot(chunk_hits, axis, off, CHUNK, 0) + half_dot(chunk_hits, axis, off, CHUNK, 1))
            return packed(early_chunk[axis, off] + half_dot(chunk_hits, axis, off, CHUNK, 1))

        for axis in range(2):
            for off in range(4):
                take(axis, 0, off)
        for axis in range(2):
            for off in SIDES + (0,):
                early[axis, off] = half_dot(slot_hits, axis, off, SLOTS, 0)
        if not first_step:
            for axis in range(2):
                for off in SIDES + (0,):
                    early_chunk[axis, off] = half_dot(chunk_hits, axis, off, CHUNK, 0)
        for axis in range(2):
            for off in (0, 3, 1, 2):
                block = gathered.at[step, axis, 1, off]
                slot = (0, step, axis, 1, off)
                remote(block, block, gather_send.at[slot], gather_recv.at[slot], sibling).wait_recv()
                take(axis, 1, off)

        line_scalars = tree4([gathered[step, 0, 0, off, pl.ds(HALF, 8), :] for off in range(4)])
        line_scalars = line_scalars + tree4([gathered[step, 0, 1, off, pl.ds(HALF, 8), :] for off in range(4)])

        for axis in range(2):
            for off in SIDES:
                sums_out[step, axis, off, pl.ds(0, HALF), :] = slot_sums(axis, off)
                sums_out[step, axis, off, pl.ds(HALF, 8), :] = line_scalars
                slot = (step, axis, (-off) % 4)
                copy = remote(
                    sums_out.at[step, axis, off],
                    sums_in.at[slot],
                    sums_send.at[slot],
                    sums_recv.at[slot],
                    line(1 - axis, off),
                )
                copy.start()
                sent.append(copy)
        if first_step:
            mark_chunks()
        for axis in range(2):
            for off in SIDES:
                chunk_out[step, axis, off] = chunk_part(axis, off)
                slot = (step, axis, (-off) % 4)
                copy = remote(
                    chunk_out.at[step, axis, off],
                    chunk_in.at[slot],
                    chunk_send.at[slot],
                    chunk_recv.at[slot],
                    line(1 - axis, off),
                )
                copy.start()
                sent.append(copy)
        for axis in range(2):
            sums_out[step, axis, 0, pl.ds(0, HALF), :] = slot_sums(axis, 0)
            sums_out[step, axis, 0, pl.ds(HALF, 8), :] = line_scalars
            chunk_out[step, axis, 0] = chunk_part(axis, 0)
        if not first_step:
            dense_three(0, dense_first, (0, 3, 1, 2))
        totals = []
        for axis in range(2):
            for off in (3, 1, 2):
                block = sums_in.at[step, axis, off]
                slot = (step, axis, off)
                remote(block, block, sums_send.at[slot], sums_recv.at[slot], sibling).wait_recv()
            totals.append(tree4([sums_out[step, axis, 0]] + [sums_in[step, axis, off] for off in (1, 2, 3)]))
        mine = jnp.concatenate(lane_swap(totals[0][:HALF], totals[1][:HALF]), axis=0)
        return mine, totals[0][HALF:]

    def chunk_sums(step):
        totals = []
        for axis in range(2):
            for off in (3, 1, 2):
                block = chunk_in.at[step, axis, off]
                slot = (step, axis, off)
                remote(block, block, chunk_send.at[slot], chunk_recv.at[slot], sibling).wait_recv()
            totals.append(tree4([chunk_out[step, axis, 0]] + [chunk_in[step, axis, off] for off in (1, 2, 3)]))
        return jnp.concatenate(lane_swap(totals[0], totals[1]), axis=0)

    def dense_one(step, dense, chunk):
        chunk_buf[step] = chunk
        own = pltpu.make_async_copy(chunk_buf.at[step], dense.at[at_x, at_z, core], own_sem.at[step])
        own.start()
        for along in range(2):
            for side in SIDES:
                span = pl.ds(along * (CHUNK // 2), CHUNK // 2)
                block = dense.at[at_x, at_z, core, span]
                slot = (step, 0, along, (-side) % 4)
                device = peer(0, side) if along else peer(side, 0)
                copy = remote(chunk_buf.at[step, span], block, dense_send.at[slot], dense_recv.at[slot], device)
                copy.start()
                sent.append(copy)
        own.wait()

    def dense_two(step, dense):
        for along in range(2):
            span = pl.ds(along * (CHUNK // 2), CHUNK // 2)
            for off in (3, 1, 2):
                if along:
                    block = dense.at[at_x, (at_z + off) % 4, core, span]
                else:
                    block = dense.at[(at_x + off) % 4, at_z, core, span]
                remote(
                    block, block, dense_send.at[step, 0, along, off], dense_recv.at[step, 0, along, off], sibling
                ).wait_recv()
        for along in range(2):
            span = pl.ds(along * (CHUNK // 2), CHUNK // 2)
            for side in SIDES:
                block = dense.at[at_x, :, core, span] if along else dense.at[:, at_z, core, span]
                device = peer(side, 0) if along else peer(0, side)
                slot = (step, 1, along, (-side) % 4)
                copy = remote(block, block, dense_send.at[slot], dense_recv.at[slot], device)
                copy.start()
                sent.append(copy)

    def dense_three(step, dense, offs):
        for off in offs:
            for along in range(2):
                span = pl.ds(along * (CHUNK // 2), CHUNK // 2)
                if off == 0:
                    slot = (step, 2, along, 0)
                    block = dense.at[at_x, :, core, span] if along else dense.at[:, at_z, core, span]
                else:
                    slot = (step, 1, along, off)
                    if along:
                        block = dense.at[(at_x + off) % 4, :, core, span]
                    else:
                        block = dense.at[:, (at_z + off) % 4, core, span]
                    remote(block, block, dense_send.at[slot], dense_recv.at[slot], sibling).wait_recv()
                    slot = (step, 2, along, off)
                copy = remote(block, block, dense_send.at[slot], dense_recv.at[slot], sibling)
                copy.start()
                sent.append(copy)

    def dense_done(step, dense):
        for off in range(4):
            for along in range(2):
                span = pl.ds(along * (CHUNK // 2), CHUNK // 2)
                if along:
                    block = dense.at[(at_x + off) % 4, :, 1 - core, span]
                else:
                    block = dense.at[:, (at_z + off) % 4, 1 - core, span]
                slot = (step, 2, along, off)
                remote(block, block, dense_send.at[slot], dense_recv.at[slot], sibling).wait_recv()

    def image_start(step, image, scalars):
        image_out[step, pl.ds(0, ROW_BLOCKS), :] = image
        image_out[step, pl.ds(ROW_BLOCKS, 8), :] = scalar_rows(scalars)
        for side in SIDES:
            back = (-side) % 4
            copy = remote(
                image_out.at[step],
                image_in.at[step, back],
                image_send.at[step, back],
                image_recv.at[step, back],
                peer(0, 0, 0, side),
            )
            copy.start()
            sent.append(copy)

    def image_finish(step):
        for off in (3, 1, 2):
            block = image_in.at[step, off]
            remote(block, block, image_send.at[step, off], image_recv.at[step, off], sibling).wait_recv()
        parts = [image_out[step]] + [image_in[step, off] for off in (1, 2, 3)]
        total = tree4(parts)
        return total[:ROW_BLOCKS], total[ROW_BLOCKS:]

    def norm_sum(scalars, between):
        value = scalar_rows(scalars)
        norm_out[...] = value
        offs = [(x, z, c) for x in (2, 1, 3, 0) for z in (2, 1, 3, 0) for c in (1, 0) if (x, z, c) != (0, 0, 0)]
        for x, z, c in offs:
            slot = ((-x) % 4, (-z) % 4, c)
            copy = remote(norm_out, norm_in.at[slot], norm_send.at[slot], norm_recv.at[slot], peer(x, z, c))
            copy.start()
            sent.append(copy)
        between()
        for slot in offs:
            block = norm_in.at[slot]
            remote(block, block, norm_send.at[slot], norm_recv.at[slot], sibling).wait_recv()
        parts = {slot: norm_in[slot] for slot in offs}
        parts[0, 0, 0] = value
        lines = [
            tree4([tree4([parts[x, z, c] for x in range(4)]) for z in range(4)]) for c in range(2)
        ]
        return lines[0] + lines[1]

    def root(square):
        return jnp.sqrt(jnp.maximum(square, 0.0) + norm_eps)

    delays = delays_ref[...]
    pick_rows(delays)
    sums, scalars = back_and_gather(0, [total_of(delays * delays)], True)
    beta_first = root(scalars[0:1])
    right_first = sums / beta_first
    left_first = delays / beta_first

    def finish_first():
        chunk = chunk_sums(0) / beta_first
        dense_one(0, dense_first, chunk)
        return chunk

    image, chunk_first = forward(right_first, finish_first)
    image_start(0, image, [total_of(chunk_first * chunk_first)])
    dense_two(0, dense_first)
    image, scalars = image_finish(0)
    alpha_part = scalars[0:1, 0:1]

    pick_rows(image)
    scalars = [alpha_part, total_of(image * image), total_of(image * left_first), total_of(left_first * left_first)]
    sums, scalars = back_and_gather(1, scalars, False)
    alpha_first = root(scalars[0:1])
    beta_second = root(
        scalars[1:2] / (alpha_first * alpha_first) - 2.0 * scalars[2:3] + alpha_first * alpha_first * scalars[3:4]
    )
    left_second = (image / alpha_first - alpha_first * left_first) / beta_second

    def second_right(back, right):
        fresh = (back / alpha_first - alpha_first * right) / beta_second
        return fresh - beta_second * (right / alpha_first)

    def finish_second():
        chunk = second_right(chunk_sums(1), chunk_first)
        dense_one(1, dense_second, chunk)
        return chunk

    image, chunk_second = forward(second_right(sums, right_first), finish_second)
    image_start(1, image, [total_of(chunk_second * chunk_second)])
    dense_two(1, dense_second)
    image, scalars = image_finish(1)
    alpha_part = scalars[0:1, 0:1]
    scalars = [alpha_part, total_of(image * image), total_of(image * left_second), total_of(left_second * left_second)]
    scalars = norm_sum(scalars, lambda: dense_three(1, dense_second, (0, 3, 1, 2)))
    alpha_second = root(scalars[0:1])
    beta_third = root(
        scalars[1:2] / (alpha_second * alpha_second) - 2.0 * scalars[2:3] + alpha_second * alpha_second * scalars[3:4]
    )
    left_ref[...] = (image / alpha_second - alpha_second * left_second) / beta_third

    rho_first = jnp.sqrt(alpha_first * alpha_first + beta_second * beta_second)
    cosine = alpha_first / rho_first
    sine = beta_second / rho_first
    step_first = cosine * beta_first / rho_first
    phi_bar = sine * beta_first
    theta = sine * alpha_second
    rho_bar = -cosine * alpha_second
    rho_second = jnp.sqrt(rho_bar * rho_bar + beta_third * beta_third)
    step_second = rho_bar / rho_second * phi_bar / rho_second
    weight_first = (step_first - step_second * (theta / rho_first)) / alpha_first
    weight_second = step_second / alpha_second

    dense_done(0, dense_first)
    dense_done(1, dense_second)
    weights_ref[...] = scalar_rows([weight_first, weight_second])
    for copy in sent:
        copy.wait_send()


def combine_kernel(first, second, weights, left, slow_hbm, left_hbm, buffer, sems):
    copies = [pltpu.make_async_copy(left, left_hbm, sems.at[4])]
    copies[0].start()
    weight_first, weight_second = weights[0:1, :], weights[1:2, :]
    for off in range(4):
        for to_z in range(4):
            buffer[off, to_z] = first[off, to_z] * weight_first + second[off, to_z] * weight_second
        copy = pltpu.make_async_copy(buffer.at[off], slow_hbm.at[off], sems.at[off])
        copy.start()
        copies.append(copy)
    for copy in copies:
        copy.wait()


def shards(delays, kernel_tiles, row_blocks, col_blocks, tile_counts):
    dma = pltpu.SemaphoreType.DMA
    vmem = pl.BlockSpec(memory_space=pltpu.VMEM)
    hbm = pl.BlockSpec(memory_space=pltpu.HBM)
    anywhere = pl.BlockSpec(memory_space=pl.ANY)
    dense_shape = (4, 4, 2, CHUNK, TILE)
    first, second, weights, left = pl.pallas_call(
        lsqr_kernel,
        out_shape=(
            jax.ShapeDtypeStruct(dense_shape, F32),
            jax.ShapeDtypeStruct(dense_shape, F32),
            jax.ShapeDtypeStruct((8, TILE), F32),
            jax.ShapeDtypeStruct((ROW_BLOCKS, TILE), F32),
        ),
        in_specs=[pl.BlockSpec(memory_space=pltpu.SMEM)] + [hbm] * 4,
        out_specs=(anywhere, anywhere, vmem, vmem),
        scratch_shapes=[
            pltpu.VMEM((ROW_BLOCKS, TILE), F32),
            pltpu.VMEM((2, HALF), jnp.int32),
            pltpu.VMEM((2, HALF), jnp.int32),
            pltpu.VMEM((SLOTS * TILE, TILE), BF16),
            pltpu.VMEM((SLOTS, 2 * TILE), F32),
            pltpu.VMEM((SLOTS, TILE), F32),
            pltpu.VMEM((2, 2, 2, 4, BLOCK_ROWS, TILE), F32),
            pltpu.VMEM((2, 4 * SLOTS, TILE), F32),
            pltpu.VMEM((2, 4 * SLOTS, 8 * SLOTS), BF16),
            pltpu.VMEM((2, 4 * CHUNK, 8 * SLOTS), BF16),
            pltpu.VMEM((2, 8 * SLOTS, TILE), BF16),
            pltpu.VMEM((2, 4, SLOTS, TILE), F32),
            pltpu.VMEM((2, 4, CHUNK, TILE), F32),
            pltpu.VMEM((SLOTS, TILE), BF16),
            pltpu.VMEM((ROW_BLOCKS, SLOTS), BF16),
            pltpu.VMEM((2, 2, 4, 8, TILE), F32),
            pltpu.VMEM((2, 2, 4, BLOCK_ROWS, TILE), F32),
            pltpu.VMEM((2, 2, 4, BLOCK_ROWS, TILE), F32),
            pltpu.VMEM((2, 2, 4, CHUNK // 2, TILE), F32),
            pltpu.VMEM((2, 2, 4, CHUNK // 2, TILE), F32),
            pltpu.VMEM((2, ROW_BLOCKS + 8, TILE), F32),
            pltpu.VMEM((2, 4, ROW_BLOCKS + 8, TILE), F32),
            pltpu.VMEM((8, TILE), F32),
            pltpu.VMEM((4, 4, 2, 8, TILE), F32),
            pltpu.VMEM((2, CHUNK, TILE), F32),
            dma((LOAD_CHUNKS,)),
            dma((3,)),
            dma((2,)),
            dma((2, 2, 2, 2, 4)),
            dma((2, 2, 2, 2, 4)),
            dma((2, 2, 4)),
            dma((2, 2, 4)),
            dma((2, 2, 4)),
            dma((2, 2, 4)),
            dma((2, 2, 4)),
            dma((2, 2, 4)),
            dma((2, 4)),
            dma((2, 4)),
            dma((4, 4, 2)),
            dma((4, 4, 2)),
            dma((2, 3, 2, 4)),
            dma((2, 3, 2, 4)),
        ],
        compiler_params=pltpu.CompilerParams(
            collective_id=0, has_side_effects=True, vmem_limit_bytes=48 * 2**20
        ),
        cost_estimate=pl.CostEstimate(flops=2 * 10**9, bytes_accessed=12 * 2**20, transcendentals=0),
    )(
        tile_counts,
        delays.reshape(ROW_BLOCKS, TILE),
        row_blocks.reshape(2, HALF),
        col_blocks.reshape(2, HALF),
        kernel_tiles.reshape(SLOTS * TILE, TILE),
    )
    slowness, left = pl.pallas_call(
        combine_kernel,
        out_shape=(
            jax.ShapeDtypeStruct(dense_shape, F32),
            jax.ShapeDtypeStruct((ROW_BLOCKS, TILE), F32),
        ),
        in_specs=[vmem] * 4,
        out_specs=(anywhere, anywhere),
        scratch_shapes=[pltpu.VMEM(dense_shape, F32), dma((5,))],
        compiler_params=pltpu.CompilerParams(vmem_limit_bytes=8 * 2**20),
        cost_estimate=pl.CostEstimate(flops=2**20, bytes_accessed=6 * 2**20, transcendentals=0),
    )(first, second, weights, left)
    return slowness.reshape(-1), left.reshape(-1)


def solution(mesh):
    in_specs = (
        P("dp"),
        P("dp", "mp", None, None, None),
        P("dp", "mp", None),
        P("dp", "mp", None),
        P("dp", "mp"),
    )
    out_specs = (P("mp"), P("dp"))
    return jax.shard_map(shards, mesh=mesh, in_specs=in_specs, out_specs=out_specs, check_vma=False)
```

```python
import jax
import jax.numpy as jnp
from jax import lax
from jax.experimental import pallas as pl
from jax.experimental.pallas import tpu as pltpu
from jax.sharding import PartitionSpec as P

TILE = 128
SLOTS = 256
HALF = SLOTS // 2
ROW_BLOCKS = 64
CELL_BLOCKS = 4096
CHUNK = CELL_BLOCKS // 32
BLOCK_ROWS = HALF + 8
GROUP = 8
LOAD_CHUNKS = 8
norm_eps = 1e-06

MESH = pl.DeviceIdType.MESH
F32 = jnp.float32
BF16 = jnp.bfloat16
NT = (((1,), (1,)), ((), ()))

SIDES = (2, 1, 3)


def split_parts(values):
    high = values.astype(BF16)
    low = (values - high.astype(F32)).astype(BF16)
    return high, low


def side_by_side(values):
    return jnp.concatenate(split_parts(values), axis=1)


def total_of(values):
    return jnp.sum(jnp.sum(values, axis=0, keepdims=True), axis=1, keepdims=True)


def tree4(parts):
    return (parts[0] + parts[2]) + (parts[1] + parts[3])


def lsqr_kernel(
    count_ref,
    delays_hbm,
    rows_hbm,
    cols_hbm,
    tiles_hbm,
    dense_first,
    dense_second,
    weights_ref,
    left_ref,
    delays_ref,
    rows_ref,
    cols_ref,
    tiles,
    picked,
    slot_products,
    gathered,
    targets,
    slot_hits,
    chunk_hits,
    rhs,
    early,
    early_chunk,
    row_pick,
    row_sum,
    cols_line,
    sums_out,
    sums_in,
    chunk_out,
    chunk_in,
    image_out,
    image_in,
    norm_out,
    norm_in,
    chunk_buf,
    load_sem,
    small_sem,
    own_sem,
    gather_send,
    gather_recv,
    cols_send,
    cols_recv,
    sums_send,
    sums_recv,
    chunk_send,
    chunk_recv,
    image_send,
    image_recv,
    norm_send,
    norm_recv,
    dense_send,
    dense_recv,
):
    dp = lax.axis_index("dp")
    mp = lax.axis_index("mp")
    at_x, at_z, core = dp // 8, (dp // 2) % 4, dp % 2

    def peer(off_x, off_z, off_core=0, off_y=0):
        there = ((at_x + off_x) % 4) * 8 + ((at_z + off_z) % 4) * 2 + (core + off_core) % 2
        return (there, (mp + off_y) % 4)

    sibling = peer(0, 0, 1)

    def remote(src, dst, send, recv, device):
        return pltpu.make_async_remote_copy(
            src_ref=src, dst_ref=dst, send_sem=send, recv_sem=recv, device_id=device, device_id_type=MESH
        )

    smalls = []
    for number, (src, dst) in enumerate(((delays_hbm, delays_ref), (rows_hbm, rows_ref), (cols_hbm, cols_ref))):
        small = pltpu.make_async_copy(src, dst, small_sem.at[number])
        small.start()
        smalls.append(small)
    load_rows = SLOTS * TILE // LOAD_CHUNKS
    loads = [None] * LOAD_CHUNKS
    for part in [p for q in range(LOAD_CHUNKS // 2) for p in (q, q + LOAD_CHUNKS // 2)]:
        span = pl.ds(part * load_rows, load_rows)
        load = pltpu.make_async_copy(tiles_hbm.at[span], tiles.at[span], load_sem.at[part])
        load.start()
        loads[part] = load

    barrier = pltpu.get_barrier_semaphore()
    partners = [peer(side, 0) for side in SIDES] + [peer(0, side) for side in SIDES]
    partners += [sibling] + [peer(0, 0, 0, side) for side in SIDES]
    for partner in partners:
        pl.semaphore_signal(barrier, inc=1, device_id=partner, device_id_type=MESH)

    sent = []

    low_lanes = lax.broadcasted_iota(jnp.int32, (TILE, TILE), 1) < TILE // 2
    lane_f = lax.broadcasted_iota(jnp.int32, (TILE, TILE), 1).astype(F32)
    sub_i = lax.broadcasted_iota(jnp.int32, (TILE, TILE), 0)

    def lane_swap(first, second):
        low = low_lanes[: first.shape[0]]
        return (
            jnp.where(low, first, pltpu.roll(second, TILE // 2, 1)),
            jnp.where(low, pltpu.roll(first, TILE // 2, 1), second),
        )

    for small in smalls:
        small.wait()
    count = count_ref[0, 0]
    rows_f = rows_ref[...].astype(F32)
    cols_f = cols_ref[...].astype(F32)
    for half in range(2):
        down = jnp.transpose(jnp.broadcast_to(rows_f[half : half + 1, :], (TILE, TILE)))
        live = sub_i + half * HALF < count
        row_pick[pl.ds(half * HALF, HALF), :] = jnp.where((down == lane_f) & live, 1.0, 0.0).astype(BF16)
        across = jnp.broadcast_to(rows_f[half : half + 1, :], (ROW_BLOCKS, TILE))
        sub_r = lax.broadcasted_iota(jnp.int32, (ROW_BLOCKS, TILE), 0).astype(F32)
        lane_r = lax.broadcasted_iota(jnp.int32, (ROW_BLOCKS, TILE), 1) + half * HALF
        row_sum[:, pl.ds(half * HALF, HALF)] = jnp.where((across == sub_r) & (lane_r < count), 1.0, 0.0).astype(BF16)
    own_cols = jnp.concatenate([cols_f, jnp.zeros((6, TILE), F32)], axis=0)
    for axis in range(2):
        cols_line[axis, 0, 0] = own_cols

    def slot_targets(axis):
        wanted = jnp.concatenate([cols_line[1 - axis, 0, off, pl.ds(0, 2), :] for off in range(4)], axis=0)
        down = jnp.transpose(jnp.concatenate([wanted, jnp.zeros((TILE - 8, TILE), F32)], axis=0))
        for part in range(8):
            targets[axis, pl.ds(part * HALF, HALF), :] = jnp.broadcast_to(down[:, part : part + 1], (HALF, TILE))

    def pick_rows(vector):
        padded = jnp.concatenate([vector, jnp.zeros((TILE - ROW_BLOCKS, TILE), F32)], axis=0)
        picked[...] = jnp.dot(row_pick[...], side_by_side(padded), preferred_element_type=F32)

    row_in_group = lax.broadcasted_iota(jnp.int32, (2 * GROUP, TILE), 0) % GROUP
    sub_group = lax.broadcasted_iota(jnp.int32, (GROUP, TILE), 0)

    def both_parts(group):
        span = pl.ds(group * GROUP, GROUP)
        return jnp.concatenate([picked[span, pl.ds(0, TILE)], picked[span, pl.ds(TILE, TILE)]], axis=0)

    def back_group(group):
        parts = both_parts(group)
        lhs = jnp.concatenate(
            [jnp.where(row_in_group == slot, parts, 0.0).astype(BF16) for slot in range(GROUP)], axis=1
        )
        weights = tiles[pl.ds(group * (GROUP * TILE), GROUP * TILE), :]
        out = jnp.dot(lhs, weights, preferred_element_type=F32)
        return out[:GROUP] + out[GROUP:]

    def forward_group(group):
        lhs = both_parts(group).astype(BF16)
        weights = tiles[pl.ds(group * (GROUP * TILE), GROUP * TILE), :]
        out = lax.dot_general(lhs, weights, NT, preferred_element_type=F32)
        out = out[:GROUP] + out[GROUP:]
        chosen = out[:, :TILE]
        for slot in range(1, GROUP):
            chosen = jnp.where(sub_group == slot, out[:, slot * TILE : (slot + 1) * TILE], chosen)
        slot_products[pl.ds(group * GROUP, GROUP), :] = chosen

    def forward(right, between, cut):
        high, low = split_parts(right)
        picked[:, pl.ds(0, TILE)] = high.astype(F32)
        picked[:, pl.ds(TILE, TILE)] = low.astype(F32)
        groups = SLOTS // GROUP

        @pl.loop(0, cut, unroll=4)
        def _(group):
            forward_group(group)

        result = between()

        @pl.loop(cut, groups, unroll=4)
        def _(group):
            forward_group(group)

        out = jnp.dot(row_sum[...], side_by_side(slot_products[...]), preferred_element_type=F32)
        return out[:, :TILE] + out[:, TILE:], result

    def scalar_rows(scalars):
        rows = [jnp.broadcast_to(value, (1, TILE)) for value in scalars]
        rows += [jnp.zeros((8 - len(rows), TILE), F32)]
        return jnp.concatenate(rows, axis=0)

    def line(axis, off, core_off=0):
        return peer(0, off, core_off) if axis else peer(off, 0, core_off)

    def exchange_cols():
        copies = []
        for axis in range(2):
            for side in SIDES:
                back = (-side) % 4
                copy = remote(
                    cols_line.at[axis, 0, 0],
                    cols_line.at[axis, 0, back],
                    cols_send.at[axis, 0, back],
                    cols_recv.at[axis, 0, back],
                    line(axis, side),
                )
                copy.start()
                copies.append(copy)
        sent.extend(copies)
        return copies

    def mark(dst, axis, span, want, core_off):
        for off in range(4):
            for half in range(2):
                one = cols_line[axis, core_off, off, pl.ds(half, 1), :]
                column = ((core_off * 4 + off) * 2 + half) * HALF
                dst[axis, span, pl.ds(column, HALF)] = jnp.where(want == one, 1.0, 0.0).astype(BF16)

    def mark_slots(core_off):
        for axis in range(2):

            @pl.loop(0, 4 * SLOTS // TILE)
            def _(part):
                span = pl.ds(part * TILE, TILE)
                mark(slot_hits, axis, span, targets[axis, span, :], core_off)

    def mark_chunks():
        for axis in range(2):

            @pl.loop(0, 4)
            def _(off):
                device = peer(off, 0)[0] if axis else peer(0, off)[0]
                want = (sub_i + device * CHUNK).astype(F32)
                for core_off in range(2):
                    mark(chunk_hits, axis, pl.ds(off * CHUNK, CHUNK), want, core_off)

    def spread_cols(copies):
        for copy in copies:
            copy.wait_recv()
        across = []
        for axis in range(2):
            copy = remote(
                cols_line.at[axis, 0], cols_line.at[axis, 1], cols_send.at[axis, 1, 0], cols_recv.at[axis, 1, 0], sibling
            )
            copy.start()
            across.append(copy)
        sent.extend(across)
        for axis in range(2):
            slot_targets(axis)
        mark_slots(0)
        for copy in across:
            copy.wait_recv()
        mark_slots(1)

    def back_and_gather(step, scalars, first_step):
        def arrival(axis, off, piece):
            span = (pl.ds(0, HALF // 2), pl.ds(HALF // 2, BLOCK_ROWS - HALF // 2))[piece]
            block = gathered.at[step, axis, 0, off, span]
            slot = (piece, step, axis, 0, off)
            return remote(block, block, gather_send.at[slot], gather_recv.at[slot], sibling)

        tail = scalar_rows(scalars)
        for axis in range(2):
            gathered[step, axis, 0, 0, pl.ds(HALF, 8), :] = tail
        chunks = LOAD_CHUNKS // 2
        groups = HALF // GROUP
        per = groups // chunks
        def send(axis, to_off, device, piece):
            span = (pl.ds(0, HALF // 2), pl.ds(HALF // 2, BLOCK_ROWS - HALF // 2))[piece]
            copy = remote(
                gathered.at[step, axis, 0, 0, span],
                gathered.at[step, axis, 0, to_off, span],
                gather_send.at[piece, step, axis, 0, to_off],
                gather_recv.at[piece, step, axis, 0, to_off],
                device,
            )
            copy.start()
            sent.append(copy)

        def across(axis, off):
            block = gathered.at[step, axis, 0, off]
            slot = (0, step, axis, 1, off)
            copy = remote(block, gathered.at[step, axis, 1, off], gather_send.at[slot], gather_recv.at[slot], sibling)
            copy.start()
            sent.append(copy)

        for part in range(chunks):
            if first_step:
                loads[part].wait()
                loads[chunks + part].wait()

            @pl.loop(0, per, unroll=per)
            def _(index):
                group = part * per + index
                low, high = lane_swap(back_group(group), back_group(groups + group))
                span = pl.ds(group * GROUP, GROUP)
                gathered[step, 0, 0, 0, span, :] = low
                gathered[step, 1, 0, 0, span, :] = high

            if 2 * (part + 1) % chunks == 0:
                piece = 2 * (part + 1) // chunks - 1
                if first_step and piece == 0:
                    pl.semaphore_wait(barrier, len(partners))
                    cols_copies = exchange_cols()
                for side in SIDES:
                    for axis in range(2):
                        send(axis, (-side) % 4, line(axis, side), piece)
        for axis in range(2):
            across(axis, 0)
        if first_step:
            spread_cols(cols_copies)
        for off in (3, 1, 2):
            for axis in range(2):
                for piece in range(2):
                    arrival(axis, off, piece).wait_recv()
                across(axis, off)

        def take(axis, core_off, off):
            block = gathered[step, axis, core_off, off, pl.ds(0, HALF), :]
            high = block.astype(BF16).astype(F32)
            first, second = lane_swap(high, block - high)
            row = (core_off * 4 + off) * SLOTS
            rhs[axis, pl.ds(row, HALF), :] = first.astype(BF16)
            rhs[axis, pl.ds(row + HALF, HALF), :] = second.astype(BF16)

        def half_dot(hits, axis, off, size, part):
            span = pl.ds(part * (4 * SLOTS), 4 * SLOTS)
            return jnp.dot(hits[axis, pl.ds(off * size, size), span], rhs[axis, span, :], preferred_element_type=F32)

        def packed(out):
            size = out.shape[0]
            out = out + pltpu.roll(out, TILE // 2, 1)
            return jnp.where(low_lanes[: size // 2], out[: size // 2], out[size // 2 :])

        def slot_sums(axis, off):
            return packed(early[axis, off] + half_dot(slot_hits, axis, off, SLOTS, 1))

        def chunk_part(axis, off):
            if first_step:
                return packed(half_dot(chunk_hits, axis, off, CHUNK, 0) + half_dot(chunk_hits, axis, off, CHUNK, 1))
            return packed(early_chunk[axis, off] + half_dot(chunk_hits, axis, off, CHUNK, 1))

        for axis in range(2):
            for off in range(4):
                take(axis, 0, off)
        for axis in range(2):
            for off in SIDES + (0,):
                early[axis, off] = half_dot(slot_hits, axis, off, SLOTS, 0)
        if not first_step:
            for axis in range(2):
                for off in SIDES + (0,):
                    early_chunk[axis, off] = half_dot(chunk_hits, axis, off, CHUNK, 0)
        for axis in range(2):
            for off in (0, 3, 1, 2):
                block = gathered.at[step, axis, 1, off]
                slot = (0, step, axis, 1, off)
                remote(block, block, gather_send.at[slot], gather_recv.at[slot], sibling).wait_recv()
                take(axis, 1, off)

        line_scalars = tree4([gathered[step, 0, 0, off, pl.ds(HALF, 8), :] for off in range(4)])
        line_scalars = line_scalars + tree4([gathered[step, 0, 1, off, pl.ds(HALF, 8), :] for off in range(4)])

        for axis in range(2):
            for off in SIDES:
                sums_out[step, axis, off, pl.ds(0, HALF), :] = slot_sums(axis, off)
                sums_out[step, axis, off, pl.ds(HALF, 8), :] = line_scalars
                slot = (step, axis, (-off) % 4)
                copy = remote(
                    sums_out.at[step, axis, off],
                    sums_in.at[slot],
                    sums_send.at[slot],
                    sums_recv.at[slot],
                    line(1 - axis, off),
                )
                copy.start()
                sent.append(copy)
        if first_step:
            mark_chunks()
        for axis in range(2):
            for off in SIDES:
                chunk_out[step, axis, off] = chunk_part(axis, off)
                slot = (step, axis, (-off) % 4)
                copy = remote(
                    chunk_out.at[step, axis, off],
                    chunk_in.at[slot],
                    chunk_send.at[slot],
                    chunk_recv.at[slot],
                    line(1 - axis, off),
                )
                copy.start()
                sent.append(copy)
        for axis in range(2):
            sums_out[step, axis, 0, pl.ds(0, HALF), :] = slot_sums(axis, 0)
            sums_out[step, axis, 0, pl.ds(HALF, 8), :] = line_scalars
            chunk_out[step, axis, 0] = chunk_part(axis, 0)
        if not first_step:
            dense_three(0, dense_first, (0, 3, 1, 2))
        totals = []
        for axis in range(2):
            for off in (3, 1, 2):
                block = sums_in.at[step, axis, off]
                slot = (step, axis, off)
                remote(block, block, sums_send.at[slot], sums_recv.at[slot], sibling).wait_recv()
            totals.append(tree4([sums_out[step, axis, 0]] + [sums_in[step, axis, off] for off in (1, 2, 3)]))
        mine = jnp.concatenate(lane_swap(totals[0][:HALF], totals[1][:HALF]), axis=0)
        return mine, totals[0][HALF:]

    def chunk_sums(step):
        totals = []
        for axis in range(2):
            for off in (3, 1, 2):
                block = chunk_in.at[step, axis, off]
                slot = (step, axis, off)
                remote(block, block, chunk_send.at[slot], chunk_recv.at[slot], sibling).wait_recv()
            totals.append(tree4([chunk_out[step, axis, 0]] + [chunk_in[step, axis, off] for off in (1, 2, 3)]))
        return jnp.concatenate(lane_swap(totals[0], totals[1]), axis=0)

    def dense_one(step, dense, chunk):
        chunk_buf[step] = chunk
        own = pltpu.make_async_copy(chunk_buf.at[step], dense.at[at_x, at_z, core], own_sem.at[step])
        own.start()
        for along in range(2):
            for side in SIDES:
                span = pl.ds(along * (CHUNK // 2), CHUNK // 2)
                block = dense.at[at_x, at_z, core, span]
                slot = (step, 0, along, (-side) % 4)
                device = peer(0, side) if along else peer(side, 0)
                copy = remote(chunk_buf.at[step, span], block, dense_send.at[slot], dense_recv.at[slot], device)
                copy.start()
                sent.append(copy)
        own.wait()

    def dense_two(step, dense):
        for along in range(2):
            span = pl.ds(along * (CHUNK // 2), CHUNK // 2)
            for off in (3, 1, 2):
                if along:
                    block = dense.at[at_x, (at_z + off) % 4, core, span]
                else:
                    block = dense.at[(at_x + off) % 4, at_z, core, span]
                remote(
                    block, block, dense_send.at[step, 0, along, off], dense_recv.at[step, 0, along, off], sibling
                ).wait_recv()
        for along in range(2):
            span = pl.ds(along * (CHUNK // 2), CHUNK // 2)
            for side in SIDES:
                block = dense.at[at_x, :, core, span] if along else dense.at[:, at_z, core, span]
                device = peer(side, 0) if along else peer(0, side)
                slot = (step, 1, along, (-side) % 4)
                copy = remote(block, block, dense_send.at[slot], dense_recv.at[slot], device)
                copy.start()
                sent.append(copy)

    def dense_three(step, dense, offs):
        for off in offs:
            for along in range(2):
                span = pl.ds(along * (CHUNK // 2), CHUNK // 2)
                if off == 0:
                    slot = (step, 2, along, 0)
                    block = dense.at[at_x, :, core, span] if along else dense.at[:, at_z, core, span]
                else:
                    slot = (step, 1, along, off)
                    if along:
                        block = dense.at[(at_x + off) % 4, :, core, span]
                    else:
                        block = dense.at[:, (at_z + off) % 4, core, span]
                    remote(block, block, dense_send.at[slot], dense_recv.at[slot], sibling).wait_recv()
                    slot = (step, 2, along, off)
                copy = remote(block, block, dense_send.at[slot], dense_recv.at[slot], sibling)
                copy.start()
                sent.append(copy)

    def dense_done(step, dense):
        for off in range(4):
            for along in range(2):
                span = pl.ds(along * (CHUNK // 2), CHUNK // 2)
                if along:
                    block = dense.at[(at_x + off) % 4, :, 1 - core, span]
                else:
                    block = dense.at[:, (at_z + off) % 4, 1 - core, span]
                slot = (step, 2, along, off)
                remote(block, block, dense_send.at[slot], dense_recv.at[slot], sibling).wait_recv()

    def image_start(step, image, scalars):
        image_out[step, pl.ds(0, ROW_BLOCKS), :] = image
        image_out[step, pl.ds(ROW_BLOCKS, 8), :] = scalar_rows(scalars)
        for side in SIDES:
            back = (-side) % 4
            copy = remote(
                image_out.at[step],
                image_in.at[step, back],
                image_send.at[step, back],
                image_recv.at[step, back],
                peer(0, 0, 0, side),
            )
            copy.start()
            sent.append(copy)

    def image_finish(step):
        for off in (3, 1, 2):
            block = image_in.at[step, off]
            remote(block, block, image_send.at[step, off], image_recv.at[step, off], sibling).wait_recv()
        parts = [image_out[step]] + [image_in[step, off] for off in (1, 2, 3)]
        total = tree4(parts)
        return total[:ROW_BLOCKS], total[ROW_BLOCKS:]

    def norm_sum(scalars, between):
        value = scalar_rows(scalars)
        norm_out[...] = value
        earlier = list(sent)
        sent.clear()
        offs = [(x, z, c) for x in (2, 1, 3, 0) for z in (2, 1, 3, 0) for c in (1, 0) if (x, z, c) != (0, 0, 0)]
        for x, z, c in offs:
            slot = ((-x) % 4, (-z) % 4, c)
            copy = remote(norm_out, norm_in.at[slot], norm_send.at[slot], norm_recv.at[slot], peer(x, z, c))
            copy.start()
            sent.append(copy)
        between()
        for copy in earlier:
            copy.wait_send()
        for slot in offs:
            block = norm_in.at[slot]
            remote(block, block, norm_send.at[slot], norm_recv.at[slot], sibling).wait_recv()
        parts = {slot: norm_in[slot] for slot in offs}
        parts[0, 0, 0] = value
        lines = [
            tree4([tree4([parts[x, z, c] for x in range(4)]) for z in range(4)]) for c in range(2)
        ]
        return lines[0] + lines[1]

    def root(square):
        return jnp.sqrt(jnp.maximum(square, 0.0) + norm_eps)

    delays = delays_ref[...]
    pick_rows(delays)
    sums, scalars = back_and_gather(0, [total_of(delays * delays)], True)
    beta_first = root(scalars[0:1])
    right_first = sums / beta_first
    left_first = delays / beta_first

    def finish_first():
        chunk = chunk_sums(0) / beta_first
        dense_one(0, dense_first, chunk)
        return chunk

    image, chunk_first = forward(right_first, finish_first, 8)
    image_start(0, image, [total_of(chunk_first * chunk_first)])
    dense_two(0, dense_first)
    image, scalars = image_finish(0)
    alpha_part = scalars[0:1, 0:1]

    pick_rows(image)
    scalars = [alpha_part, total_of(image * image), total_of(image * left_first), total_of(left_first * left_first)]
    sums, scalars = back_and_gather(1, scalars, False)
    alpha_first = root(scalars[0:1])
    beta_second = root(
        scalars[1:2] / (alpha_first * alpha_first) - 2.0 * scalars[2:3] + alpha_first * alpha_first * scalars[3:4]
    )
    left_second = (image / alpha_first - alpha_first * left_first) / beta_second

    def second_right(back, right):
        fresh = (back / alpha_first - alpha_first * right) / beta_second
        return fresh - beta_second * (right / alpha_first)

    def finish_second():
        chunk = second_right(chunk_sums(1), chunk_first)
        dense_one(1, dense_second, chunk)
        return chunk

    image, chunk_second = forward(second_right(sums, right_first), finish_second, 4)
    image_start(1, image, [total_of(chunk_second * chunk_second)])
    dense_two(1, dense_second)
    image, scalars = image_finish(1)
    alpha_part = scalars[0:1, 0:1]
    scalars = [alpha_part, total_of(image * image), total_of(image * left_second), total_of(left_second * left_second)]
    scalars = norm_sum(scalars, lambda: dense_three(1, dense_second, (0, 3, 1, 2)))
    alpha_second = root(scalars[0:1])
    beta_third = root(
        scalars[1:2] / (alpha_second * alpha_second) - 2.0 * scalars[2:3] + alpha_second * alpha_second * scalars[3:4]
    )
    left_ref[...] = (image / alpha_second - alpha_second * left_second) / beta_third

    rho_first = jnp.sqrt(alpha_first * alpha_first + beta_second * beta_second)
    cosine = alpha_first / rho_first
    sine = beta_second / rho_first
    step_first = cosine * beta_first / rho_first
    phi_bar = sine * beta_first
    theta = sine * alpha_second
    rho_bar = -cosine * alpha_second
    rho_second = jnp.sqrt(rho_bar * rho_bar + beta_third * beta_third)
    step_second = rho_bar / rho_second * phi_bar / rho_second
    weight_first = (step_first - step_second * (theta / rho_first)) / alpha_first
    weight_second = step_second / alpha_second

    dense_done(0, dense_first)
    dense_done(1, dense_second)
    weights_ref[...] = scalar_rows([weight_first, weight_second])
    for copy in sent:
        copy.wait_send()


def combine_kernel(first, second, weights, left, slow_hbm, left_hbm, buffer, sems):
    copies = [pltpu.make_async_copy(left, left_hbm, sems.at[4])]
    copies[0].start()
    weight_first, weight_second = weights[0:1, :], weights[1:2, :]
    for off in range(4):
        for to_z in range(4):
            buffer[off, to_z] = first[off, to_z] * weight_first + second[off, to_z] * weight_second
        copy = pltpu.make_async_copy(buffer.at[off], slow_hbm.at[off], sems.at[off])
        copy.start()
        copies.append(copy)
    for copy in copies:
        copy.wait()


def shards(delays, kernel_tiles, row_blocks, col_blocks, tile_counts):
    dma = pltpu.SemaphoreType.DMA
    vmem = pl.BlockSpec(memory_space=pltpu.VMEM)
    hbm = pl.BlockSpec(memory_space=pltpu.HBM)
    anywhere = pl.BlockSpec(memory_space=pl.ANY)
    dense_shape = (4, 4, 2, CHUNK, TILE)
    first, second, weights, left = pl.pallas_call(
        lsqr_kernel,
        out_shape=(
            jax.ShapeDtypeStruct(dense_shape, F32),
            jax.ShapeDtypeStruct(dense_shape, F32),
            jax.ShapeDtypeStruct((8, TILE), F32),
            jax.ShapeDtypeStruct((ROW_BLOCKS, TILE), F32),
        ),
        in_specs=[pl.BlockSpec(memory_space=pltpu.SMEM)] + [hbm] * 4,
        out_specs=(anywhere, anywhere, vmem, vmem),
        scratch_shapes=[
            pltpu.VMEM((ROW_BLOCKS, TILE), F32),
            pltpu.VMEM((2, HALF), jnp.int32),
            pltpu.VMEM((2, HALF), jnp.int32),
            pltpu.VMEM((SLOTS * TILE, TILE), BF16),
            pltpu.VMEM((SLOTS, 2 * TILE), F32),
            pltpu.VMEM((SLOTS, TILE), F32),
            pltpu.VMEM((2, 2, 2, 4, BLOCK_ROWS, TILE), F32),
            pltpu.VMEM((2, 4 * SLOTS, TILE), F32),
            pltpu.VMEM((2, 4 * SLOTS, 8 * SLOTS), BF16),
            pltpu.VMEM((2, 4 * CHUNK, 8 * SLOTS), BF16),
            pltpu.VMEM((2, 8 * SLOTS, TILE), BF16),
            pltpu.VMEM((2, 4, SLOTS, TILE), F32),
            pltpu.VMEM((2, 4, CHUNK, TILE), F32),
            pltpu.VMEM((SLOTS, TILE), BF16),
            pltpu.VMEM((ROW_BLOCKS, SLOTS), BF16),
            pltpu.VMEM((2, 2, 4, 8, TILE), F32),
            pltpu.VMEM((2, 2, 4, BLOCK_ROWS, TILE), F32),
            pltpu.VMEM((2, 2, 4, BLOCK_ROWS, TILE), F32),
            pltpu.VMEM((2, 2, 4, CHUNK // 2, TILE), F32),
            pltpu.VMEM((2, 2, 4, CHUNK // 2, TILE), F32),
            pltpu.VMEM((2, ROW_BLOCKS + 8, TILE), F32),
            pltpu.VMEM((2, 4, ROW_BLOCKS + 8, TILE), F32),
            pltpu.VMEM((8, TILE), F32),
            pltpu.VMEM((4, 4, 2, 8, TILE), F32),
            pltpu.VMEM((2, CHUNK, TILE), F32),
            dma((LOAD_CHUNKS,)),
            dma((3,)),
            dma((2,)),
            dma((2, 2, 2, 2, 4)),
            dma((2, 2, 2, 2, 4)),
            dma((2, 2, 4)),
            dma((2, 2, 4)),
            dma((2, 2, 4)),
            dma((2, 2, 4)),
            dma((2, 2, 4)),
            dma((2, 2, 4)),
            dma((2, 4)),
            dma((2, 4)),
            dma((4, 4, 2)),
            dma((4, 4, 2)),
            dma((2, 3, 2, 4)),
            dma((2, 3, 2, 4)),
        ],
        compiler_params=pltpu.CompilerParams(
            collective_id=0, has_side_effects=True, vmem_limit_bytes=48 * 2**20
        ),
        cost_estimate=pl.CostEstimate(flops=2 * 10**9, bytes_accessed=12 * 2**20, transcendentals=0),
    )(
        tile_counts,
        delays.reshape(ROW_BLOCKS, TILE),
        row_blocks.reshape(2, HALF),
        col_blocks.reshape(2, HALF),
        kernel_tiles.reshape(SLOTS * TILE, TILE),
    )
    slowness, left = pl.pallas_call(
        combine_kernel,
        out_shape=(
            jax.ShapeDtypeStruct(dense_shape, F32),
            jax.ShapeDtypeStruct((ROW_BLOCKS, TILE), F32),
        ),
        in_specs=[vmem] * 4,
        out_specs=(anywhere, anywhere),
        scratch_shapes=[pltpu.VMEM(dense_shape, F32), dma((5,))],
        compiler_params=pltpu.CompilerParams(vmem_limit_bytes=8 * 2**20),
        cost_estimate=pl.CostEstimate(flops=2**20, bytes_accessed=6 * 2**20, transcendentals=0),
    )(first, second, weights, left)
    return slowness.reshape(-1), left.reshape(-1)


def solution(mesh):
    in_specs = (
        P("dp"),
        P("dp", "mp", None, None, None),
        P("dp", "mp", None),
        P("dp", "mp", None),
        P("dp", "mp"),
    )
    out_specs = (P("mp"), P("dp"))
    return jax.shard_map(shards, mesh=mesh, in_specs=in_specs, out_specs=out_specs, check_vma=False)
```
